256 devices in a mesh: tm: 64 (over x, y, z_hi, core), grp: 4 (over z_lo).
Axes of the slice: x: 4, y: 4, z: 8 (z_hi: 2, z_lo: 4; z = z_hi * 4 + z_lo), core: 2. Of those that a mesh axis runs over, the one named last changes fastest.
Arguments:
- traces: bfloat16 [4096, 32768], P('grp', 'tm'), may hold values from -6 to 6
- fir_taps: bfloat16 [129], replicated, may hold values from -0.5 to 0.5
- gauge_half: int32 [4096], P('grp'), may hold values from 1 to 8
- sta_length: int32 [4096], P('grp'), may hold values from 8 to 16
- lta_length: int32 [4096], P('grp'), may hold values from 64 to 128
- band_edges: int32 [9], replicated, may hold values from 1 to 127, as said below
Outputs:
- trigger_ratio: bfloat16 [4, 1024, 32768], P('grp', 'tm')
- band_signature: float32 [4, 1024, 8, 128], P('grp', 'tm')
The draws below stay inside these ranges and needn't reach their ends.
Inputs may be any that keep to these rules, and one draw needn't show every extreme that they name: band_edges rises strictly; its first entry is 1 and its last 127.
All inputs are finite; a program needn't handle non-finite values.
Results may differ from the reference program's by a relative error of at most 0.0036.
Values may be sent and summed in bfloat16 or wider, within the bound.
A program may use at most 64 MiB of HBM per device.

```python
import math
import jax
import jax.numpy as jnp
from jax import lax

CHAN = 4096
NTAPS = 129
HMAX = 8
SMIN = 8
SMAX = 16
LMIN = 64
LMAX = 128
FRAME = 256
NBANDS = 8
CH_GRP = 1024
NT = 32768
NFRAMES = 128
N_GRP = 4


def draw_band_edges(key, part):
    inner = jax.random.permutation(jax.random.fold_in(key, 17), FRAME // 2 - 3)[:NBANDS - 1] + 2
    inner = jnp.sort(inner.astype(jnp.int32))
    first = jnp.ones((1,), jnp.int32)
    last = jnp.full((1,), FRAME // 2 - 1, jnp.int32)
    return jnp.concatenate([first, inner, last]).astype(jnp.int32)


def plant(array, rng, smallest, largest):
    spot = [jax.random.randint(jax.random.fold_in(rng, axis), (), 0, length) for axis, length in enumerate(array.shape)]
    widest = array.shape.index(max(array.shape))
    next_to = spot[:widest] + [(spot[widest] + 1) % array.shape[widest]] + spot[widest + 1:]
    return array.at[tuple(spot)].set(smallest).at[tuple(next_to)].set(largest)


def shard_levels(stream_key, extent, shards, low, high):
    factor_of, own = 1.0, jax.random.fold_in(stream_key, 6)
    for dim, parts in shards:
        draws = jnp.exp(jax.random.uniform(jax.random.fold_in(own, dim), (parts,), jnp.float32, low / len(shards), high / len(shards)))
        factor_of = factor_of * jnp.repeat(draws, extent[dim] // parts).reshape([-1 if axis == dim else 1 for axis in range(len(extent))])
    return factor_of


def noise(stream_key, dims, scale, limit, pieces=(), held_as=jnp.bfloat16):
    loudness = shard_levels(stream_key, dims, pieces, -0.22, 0.18) if pieces else 1.0
    values = jax.random.normal(stream_key, dims, jnp.float32) * scale * loudness
    return jnp.minimum(jnp.maximum(values, -limit), limit).astype(held_as)


def setup_inputs(seed: int = 0) -> dict:
    keys = jax.random.split(jax.random.key(seed), 7)
    traces = noise(keys[0], (CHAN, NT), 1.0, 6.0, ((0, 4), (1, 64)))
    fir_taps = noise(keys[1], (NTAPS,), NTAPS ** -0.5, 0.5)
    gauge_half = plant(jax.random.randint(keys[2], (CHAN,), 1, HMAX + 1), jax.random.fold_in(keys[2], 1), 1, HMAX).astype(jnp.int32)
    sta_length = plant(jax.random.randint(keys[3], (CHAN,), SMIN, SMAX + 1), jax.random.fold_in(keys[3], 1), SMIN, SMAX).astype(jnp.int32)
    lta_length = plant(jax.random.randint(keys[4], (CHAN,), LMIN, LMAX + 1), jax.random.fold_in(keys[4], 1), LMIN, LMAX).astype(jnp.int32)
    band_edges = draw_band_edges(jax.random.fold_in(keys[6], 71), 0)
    return {"traces": traces, "fir_taps": fir_taps, "gauge_half": gauge_half, "sta_length": sta_length, "lta_length": lta_length, "band_edges": band_edges}


def gauge_apply(extended, half_gauge):
    count = half_gauge.shape[0]
    centre = extended[HMAX:HMAX + count].astype(jnp.float32)
    sides = jnp.zeros(centre.shape, jnp.float32)
    for offset in range(1, HMAX + 1):
        paired = extended[HMAX + offset:HMAX + offset + count].astype(jnp.float32) + extended[HMAX - offset:HMAX - offset + count].astype(jnp.float32)
        sides = jnp.where((half_gauge == offset)[:, None], paired, sides)
    return (centre - 0.5 * sides).astype(jnp.bfloat16)


def window_sums(energy, lengths):
    count, total = energy.shape
    running = jnp.cumsum(energy, axis=1)
    padded = jnp.concatenate([jnp.zeros((count, LMAX), energy.dtype), running], axis=1)

    def one_row(row, length):
        return lax.dynamic_slice_in_dim(row, (LMAX - length).astype(jnp.int32), total)

    earlier = jax.vmap(one_row)(padded, lengths)
    return running - earlier


def detect(filtered, sta, lta, edges):
    count, total = filtered.shape
    energy = filtered * filtered
    short_mean = window_sums(energy, sta) / sta.astype(jnp.float32)[:, None]
    long_mean = window_sums(energy, lta) / lta.astype(jnp.float32)[:, None]
    ratio = (short_mean / jnp.maximum(long_mean, 0.5)).astype(jnp.bfloat16)
    positions = jnp.arange(FRAME).astype(jnp.float32)
    hann_window = 0.5 - 0.5 * jnp.cos(2.0 * math.pi * positions / FRAME)
    frames = filtered.reshape(count, total // FRAME, FRAME) * hann_window
    spectrum = jnp.fft.rfft(frames, axis=-1)[..., :FRAME // 2]
    power = jnp.real(spectrum) ** 2 + jnp.imag(spectrum) ** 2
    bins = jnp.arange(FRAME // 2).astype(jnp.int32)
    lower = edges[:-1]
    upper = edges[1:]
    select = ((bins[:, None] >= lower[None, :]) & (bins[:, None] < upper[None, :])).astype(jnp.float32)
    widths = (upper - lower).astype(jnp.float32)
    band = jnp.einsum('rfk,kb->rbf', power.astype(jnp.float32), select, precision=lax.Precision.HIGHEST) / widths[None, :, None]
    return ratio, jnp.log1p(band / FRAME)


def reference(traces, fir_taps, gauge_half, sta_length, lta_length, band_edges):
    padded = jnp.pad(traces, ((HMAX, HMAX), (0, 0)))
    block = min(128, CHAN)
    reach = (NTAPS - 1) // 2

    def one_block(index):
        start = (index * block).astype(jnp.int32)
        extended = lax.dynamic_slice_in_dim(padded, start, block + 2 * HMAX, 0)
        half_gauge = lax.dynamic_slice_in_dim(gauge_half, start, block)
        sta = lax.dynamic_slice_in_dim(sta_length, start, block)
        lta = lax.dynamic_slice_in_dim(lta_length, start, block)
        gauged = gauge_apply(extended, half_gauge)
        filtered = lax.conv_general_dilated(gauged.astype(jnp.float32)[:, None, :], fir_taps.astype(jnp.float32)[None, None, :], (1,), [(reach, reach)], precision=lax.Precision.HIGHEST)[:, 0, :]
        return detect(filtered, sta, lta, band_edges)

    ratio, signature = lax.map(one_block, jnp.arange(CHAN // block, dtype=jnp.int32))
    return ratio.reshape(N_GRP, CH_GRP, NT), signature.reshape(N_GRP, CH_GRP, NBANDS, NFRAMES)
```

```python
import functools
import math

import jax
import jax.numpy as jnp
import numpy as np
from jax import lax
from jax.experimental import pallas as pl
from jax.experimental.pallas import tpu as pltpu
from jax.sharding import PartitionSpec as P

NTAPS = 129
REACH = 64
LANES = 128
FRAME = 256
NBANDS = 8
ROWS = 16
MESH = pl.DeviceIdType.MESH
F32 = jnp.float32
BF16 = jnp.bfloat16


def spectral_tables():
    n = np.arange(FRAME)
    k = np.arange(FRAME // 2)
    angle = 2.0 * math.pi * ((n[:, None] * k[None, :]) % FRAME) / FRAME
    hann = 0.5 - 0.5 * np.cos(2.0 * math.pi * n / FRAME)
    table = np.concatenate([np.cos(angle), np.sin(angle)], axis=1) * hann[:, None]
    high = table.astype(jnp.bfloat16)
    low = (table - high.astype(np.float64)).astype(jnp.bfloat16)
    return high, low


def iota(shape, dim):
    return lax.broadcasted_iota(jnp.int32, shape, dim)


def split(x):
    high = x.astype(BF16)
    return high, (x - high.astype(F32)).astype(BF16)


def dot(a, b):
    return jnp.dot(a, b, preferred_element_type=F32)


def dot_nt(a, b):
    return lax.dot_general(a, b, (((1,), (1,)), ((), ())), preferred_element_type=F32)


def gauge_matrix(half, width, off):
    n = half.shape[0]
    if width > LANES:
        half = jnp.concatenate([half] * (width // LANES), axis=1)
    rel = (iota((n, width), 1) - iota((n, width), 0) - off).astype(F32)
    side = jnp.where(jnp.abs(rel) == half, -0.5, 0.0)
    return jnp.where(rel == 0.0, 1.0, side).astype(BF16)


def kernel(
    slabs, groups,
    traces, taps, half, sta, lta, edges, th, tl,
    ratio_out, sig_out,
    x, ga, r, lo_halo, hi_halo, toep, windows, sel, widths, fa, fb, ra, rb,
    in_sem, send_sem, recv_sem, hsend, hrecv,
):
    me = lax.axis_index("tm")
    g = lax.axis_index("grp")
    chans = x.shape[0]
    block = min(LANES, chans)
    per = block // ROWS
    has_lo = g > 0
    has_hi = g < groups - 1

    load = pltpu.make_async_copy(traces, x, in_sem)
    load.start()
    barrier = pltpu.get_barrier_semaphore()

    @pl.loop(1, slabs)
    def _(k):
        pl.semaphore_signal(barrier, inc=1, device_id=((me + k) % slabs, g), device_id_type=MESH)

    @pl.when(has_lo)
    def _():
        pl.semaphore_signal(barrier, inc=1, device_id=(me, g - 1), device_id_type=MESH)

    @pl.when(has_hi)
    def _():
        pl.semaphore_signal(barrier, inc=1, device_id=(me, g + 1), device_id_type=MESH)

    def half_column(i):
        row = jnp.broadcast_to(half[pl.ds(i, 1), :], (LANES, LANES))
        return row.T[:block]

    load.wait()
    width = min(2 * LANES, chans)

    @pl.loop(0, chans // block)
    def _(i):
        start = jnp.clip(i * block - REACH, 0, chans - width)
        rows = x[pl.ds(pl.multiple_of(start, ROWS), width), :]
        m = gauge_matrix(half_column(i), width, i * block - start)
        ga[pl.ds(i * per, per)] = dot(m, rows).astype(BF16).reshape(per, ROWS, x.shape[1])

    neighbours = jnp.where(has_lo, 1, 0) + jnp.where(has_hi, 1, 0)
    pl.semaphore_wait(barrier, slabs - 1 + neighbours)

    def to_hi():
        return pltpu.make_async_remote_copy(
            src_ref=traces.at[pl.ds(chans - ROWS, ROWS)], dst_ref=lo_halo, send_sem=hsend.at[0],
            recv_sem=hrecv.at[0], device_id=(me, g + 1), device_id_type=MESH)

    def to_lo():
        return pltpu.make_async_remote_copy(
            src_ref=traces.at[pl.ds(0, ROWS)], dst_ref=hi_halo, send_sem=hsend.at[1],
            recv_sem=hrecv.at[1], device_id=(me, g - 1), device_id_type=MESH)

    @pl.when(has_hi)
    def _():
        to_hi().start()

    @pl.when(has_lo)
    def _():
        to_lo().start()

    def send(d):
        return pltpu.make_async_remote_copy(
            src_ref=ga.at[d], dst_ref=r.at[me + 1], send_sem=send_sem.at[d],
            recv_sem=recv_sem.at[me], device_id=(d, g), device_id_type=MESH)

    early = min(16, slabs)

    @pl.loop(1, early)
    def _(k):
        d = (me + k) % slabs

        @pl.when(jnp.logical_and(d != 0, d != slabs - 1))
        def _():
            send(d).start()

    @pl.when(has_lo)
    def _():
        to_hi().wait_recv()

    @pl.when(jnp.logical_not(has_lo))
    def _():
        lo_halo[...] = jnp.zeros_like(lo_halo)

    @pl.when(has_hi)
    def _():
        to_lo().wait_recv()

    @pl.when(jnp.logical_not(has_hi))
    def _():
        hi_halo[...] = jnp.zeros_like(hi_halo)

    edge = min(LANES - ROWS, chans)
    first = jnp.concatenate([lo_halo[...], x[0:edge, :]], axis=0)
    m = gauge_matrix(half_column(0)[:ROWS], LANES, ROWS)[:, : edge + ROWS]
    ga[0] = dot(m, first).astype(BF16)
    last = jnp.concatenate([x[chans - edge :, :], hi_halo[...]], axis=0)
    m = gauge_matrix(half_column(chans // block - 1)[block - ROWS :], LANES, edge - ROWS)[:, : edge + ROWS]
    ga[slabs - 1] = dot(m, last).astype(BF16)

    @pl.loop(1, slabs)
    def _(k):
        d = (me + k) % slabs

        @pl.when(jnp.logical_or(k >= early, jnp.logical_or(d == 0, d == slabs - 1)))
        def _():
            send(d).start()

    r[pl.ds(me + 1, 1)] = ga[pl.ds(me, 1)]
    r[0] = jnp.zeros(r.shape[1:], BF16)
    r[slabs + 1] = jnp.zeros(r.shape[1:], BF16)
    zero = jnp.zeros((2 * ROWS, LANES), F32)
    fa[0 : 2 * ROWS] = zero
    fb[0 : 2 * ROWS] = zero
    row = jnp.broadcast_to(taps[...], (FRAME, 2 * FRAME))
    toep[...] = pltpu.roll(row, 0, 1, stride=1, stride_axis=0).astype(BF16)
    bands = iota((ROWS, LANES), 0)
    lower = jnp.zeros((ROWS, LANES), jnp.int32)
    upper = jnp.zeros((ROWS, LANES), jnp.int32)
    for b in range(NBANDS):
        lower = jnp.where(bands == b, edges[b], lower)
        upper = jnp.where(bands == b, edges[b + 1], upper)
    bins = iota((ROWS, LANES), 1)
    sel[...] = jnp.where(jnp.logical_and(bins >= lower, bins < upper), 1.0, 0.0).astype(BF16)
    widths[...] = (upper - lower).astype(F32)[:NBANDS]

    @pl.loop(0, ROWS)
    def _(c):
        back = iota((FRAME, LANES), 1) + LANES - iota((FRAME, LANES), 0)
        past = back >= 0
        short = jnp.where(jnp.logical_and(past, back < sta[me * ROWS + c]), 1.0, 0.0).astype(BF16)
        long = jnp.where(jnp.logical_and(past, back < lta[me * ROWS + c]), 1.0, 0.0).astype(BF16)
        windows[c] = jnp.concatenate([short, long], axis=1)

    @pl.loop(1, slabs)
    def _(k):
        s = (me + k) % slabs
        pltpu.make_async_remote_copy(
            src_ref=ga.at[s], dst_ref=r.at[s + 1], send_sem=send_sem.at[s],
            recv_sem=recv_sem.at[s], device_id=(s, g), device_id_type=MESH).wait_recv()

    step = min(8, slabs)
    rows = step * ROWS

    @pl.loop(0, slabs // step)
    def _(i):
        s0 = i * step

        def tile(slab, q):
            return r[pl.ds(s0 + slab, step), :, q * LANES : (q + 1) * LANES].reshape(rows, LANES)

        own = [tile(1, q) for q in range(4)]
        for f, parts in enumerate(([tile(0, 3)] + own[:3], own[1:] + [tile(2, 0)])):
            out = dot_nt(jnp.concatenate(parts, axis=1), toep[...])
            for j in range(step):
                at = pl.multiple_of(((s0 + 1 + j) * 2 + f) * ROWS, ROWS)
                fa[pl.ds(at, ROWS), :] = out[j * ROWS : (j + 1) * ROWS, :LANES]
                fb[pl.ds(at, ROWS), :] = out[j * ROWS : (j + 1) * ROWS, LANES:]

    frames = 2 * slabs

    @pl.loop(0, ROWS)
    def _(c):
        first = fa[pl.ds(2 * ROWS + c, frames, stride=ROWS), :]
        second = fb[pl.ds(2 * ROWS + c, frames, stride=ROWS), :]
        before = fb[pl.ds(ROWS + c, frames, stride=ROWS), :]
        high, low = split(jnp.concatenate([first, second], axis=1))
        spectrum = dot(high, th[...]) + (dot(low, th[...]) + dot(high, tl[...]))
        power = spectrum[:, :LANES] * spectrum[:, :LANES] + spectrum[:, LANES:] * spectrum[:, LANES:]
        high, low = split(power)
        band = (dot_nt(sel[...], high) + dot_nt(sel[...], low))[:NBANDS]
        sig_out[c] = jnp.log1p(band / widths[:, :frames] / FRAME)
        e0 = jnp.concatenate([before * before, first * first], axis=1)
        e1 = jnp.concatenate([first * first, second * second], axis=1)
        high, low = split(jnp.concatenate([e0, e1], axis=0))
        sums = dot(high, windows[c]) + dot(low, windows[c])
        count_s = jnp.full((1, LANES), sta[me * ROWS + c].astype(F32), F32)
        count_l = jnp.full((1, LANES), lta[me * ROWS + c].astype(F32), F32)
        ratio = (sums[:, :LANES] * (1.0 / count_s)) / jnp.maximum(sums[:, LANES:] * (1.0 / count_l), 0.5)
        ra[pl.ds(c, frames, stride=ROWS), :] = ratio[:frames]
        rb[pl.ds(c, frames, stride=ROWS), :] = ratio[frames:]

    @pl.loop(0, frames)
    def _(f):
        for h, ref in enumerate((ra, rb)):
            at = pl.multiple_of(f * FRAME + h * LANES, LANES)
            ratio_out[:, pl.ds(at, LANES)] = ref[pl.ds(pl.multiple_of(f * ROWS, ROWS), ROWS), :].astype(BF16)

    @pl.when(has_hi)
    def _():
        to_hi().wait_send()

    @pl.when(has_lo)
    def _():
        to_lo().wait_send()

    @pl.loop(1, slabs)
    def _(k):
        send((me + k) % slabs).wait_send()


def body(traces, fir_taps, gauge_half, sta_length, lta_length, band_edges):
    slabs, groups = lax.axis_size("tm"), lax.axis_size("grp")
    chans, local = traces.shape
    taps = jnp.pad(fir_taps.astype(F32), (REACH, 2 * FRAME - REACH - NTAPS))[None, :]
    half = gauge_half.astype(F32)
    half = (jnp.pad(half, (0, -chans % LANES))).reshape(-1, LANES)
    th, tl = (jnp.asarray(t) for t in spectral_tables())
    total = slabs * local
    vmem = pl.BlockSpec(memory_space=pltpu.VMEM)
    smem = pl.BlockSpec(memory_space=pltpu.SMEM)
    padded = (slabs + 1) * 2 * ROWS
    ratio, signature = pl.pallas_call(
        functools.partial(kernel, slabs, groups),
        out_shape=(
            jax.ShapeDtypeStruct((ROWS, total), BF16),
            jax.ShapeDtypeStruct((ROWS, NBANDS, total // FRAME), F32),
        ),
        in_specs=[pl.BlockSpec(memory_space=pl.ANY), vmem, vmem, smem, smem, smem, vmem, vmem],
        out_specs=(vmem, vmem),
        scratch_shapes=[
            pltpu.VMEM((chans, local), BF16),
            pltpu.VMEM((slabs, ROWS, local), BF16),
            pltpu.VMEM((slabs + 2, ROWS, local), BF16),
            pltpu.VMEM((ROWS, local), BF16),
            pltpu.VMEM((ROWS, local), BF16),
            pltpu.VMEM((FRAME, 2 * FRAME), BF16),
            pltpu.VMEM((ROWS, FRAME, FRAME), BF16),
            pltpu.VMEM((ROWS, LANES), BF16),
            pltpu.VMEM((NBANDS, LANES), F32),
            pltpu.VMEM((padded, LANES), F32),
            pltpu.VMEM((padded, LANES), F32),
            pltpu.VMEM((2 * slabs * ROWS, LANES), F32),
            pltpu.VMEM((2 * slabs * ROWS, LANES), F32),
            pltpu.SemaphoreType.DMA,
            pltpu.SemaphoreType.DMA((slabs,)),
            pltpu.SemaphoreType.DMA((slabs,)),
            pltpu.SemaphoreType.DMA((2,)),
            pltpu.SemaphoreType.DMA((2,)),
        ],
        compiler_params=pltpu.CompilerParams(
            collective_id=0, has_side_effects=True, vmem_limit_bytes=48 * 2**20
        ),
        cost_estimate=pl.CostEstimate(flops=4 * 10**9, bytes_accessed=3 * 2**20, transcendentals=0),
    )(traces, taps, half, sta_length, lta_length, band_edges, th, tl)
    return ratio[None], signature[None]


def solution(mesh):
    in_specs = (P("grp", "tm"), P(), P("grp"), P("grp"), P("grp"), P())
    out_specs = (P("grp", "tm", None), P("grp", "tm", None, None))
    return jax.shard_map(body, mesh=mesh, in_specs=in_specs, out_specs=out_specs, check_vma=False)
```

```python
import functools
import math

import jax
import jax.numpy as jnp
import numpy as np
from jax import lax
from jax.experimental import pallas as pl
from jax.experimental.pallas import tpu as pltpu
from jax.sharding import PartitionSpec as P

NTAPS = 129
REACH = 64
LANES = 128
FRAME = 256
NBANDS = 8
ROWS = 16
STEP = 8
MESH = pl.DeviceIdType.MESH
F32 = jnp.float32
BF16 = jnp.bfloat16


def spectral_table():
    n = np.arange(FRAME)
    k = np.arange(FRAME // 2)
    angle = 2.0 * math.pi * ((n[:, None] * k[None, :]) % FRAME) / FRAME
    hann = 0.5 - 0.5 * np.cos(2.0 * math.pi * n / FRAME)
    table = np.concatenate([np.cos(angle), np.sin(angle)], axis=1) * hann[:, None]
    high = table.astype(jnp.bfloat16)
    low = (table - high.astype(np.float64)).astype(jnp.bfloat16)
    return np.concatenate([high, high, low], axis=0)


def iota(shape, dim):
    return lax.broadcasted_iota(jnp.int32, shape, dim)


def split(x, terms):
    parts = []
    for _ in range(terms - 1):
        parts.append(x.astype(BF16))
        x = x - parts[-1].astype(F32)
    return parts + [x.astype(BF16)]


def dot(a, b):
    return jnp.dot(a, b, preferred_element_type=F32)


def lanes(*parts):
    return jnp.concatenate(parts, axis=1)


def stack(*parts):
    return jnp.concatenate(parts, axis=0)


def gauge_matrix(half, width, off):
    n = half.shape[0]
    if width > LANES:
        half = lanes(*[half] * (width // LANES))
    rel = (iota((n, width), 1) - iota((n, width), 0) - off).astype(F32)
    side = jnp.where(jnp.abs(rel) == half, -0.5, 0.0)
    return jnp.where(rel == 0.0, 1.0, side).astype(BF16)


def kernel(
    slabs, groups,
    traces, taps_in, half_in, sta_in, lta_in, edges_in, table_in,
    ratio_out, sig_out,
    x, ga, r, lo_halo, hi_halo, taps, half, table, toep, sums, sel, widths, turn, scale, bands,
    sta, lta, edges,
    in_sem, send_sem, recv_sem, hsend, hrecv,
):
    me = lax.axis_index("tm")
    g = lax.axis_index("grp")
    chans = x.shape[0]
    block = LANES
    per = block // ROWS
    columns = slabs // 4
    own = me // 4
    has_lo = g > 0
    has_hi = g < groups - 1

    pairs = [(traces, x), (half_in, half), (table_in, table), (taps_in, taps), (sta_in, sta), (lta_in, lta), (edges_in, edges)]
    loads = [pltpu.make_async_copy(a, b, in_sem.at[i]) for i, (a, b) in enumerate(pairs)]
    for load in loads:
        load.start()
    barrier = pltpu.get_barrier_semaphore()

    @pl.loop(1, slabs)
    def _(k):
        pl.semaphore_signal(barrier, inc=1, device_id=((me + k) % slabs, g), device_id_type=MESH)

    @pl.when(has_lo)
    def _():
        pl.semaphore_signal(barrier, inc=1, device_id=(me, g - 1), device_id_type=MESH)

    @pl.when(has_hi)
    def _():
        pl.semaphore_signal(barrier, inc=1, device_id=(me, g + 1), device_id_type=MESH)

    def half_column(i):
        row = jnp.broadcast_to(half[pl.ds(i, 1), :].astype(F32), (LANES, LANES))
        return row.T

    loads[0].wait()
    loads[1].wait()
    width = min(2 * LANES, chans)

    @pl.loop(0, chans // block)
    def _(i):
        start = jnp.clip(i * block - REACH, 0, chans - width)
        rows = x[pl.ds(pl.multiple_of(start, ROWS), width), :]
        m = gauge_matrix(half_column(i), width, i * block - start)
        ga[pl.ds(i * per, per)] = dot(m, rows).astype(BF16).reshape(per, ROWS, x.shape[1])

    neighbours = jnp.where(has_lo, 1, 0) + jnp.where(has_hi, 1, 0)
    pl.semaphore_wait(barrier, slabs - 1 + neighbours)

    def to_hi():
        return pltpu.make_async_remote_copy(
            src_ref=traces.at[pl.ds(chans - ROWS, ROWS)], dst_ref=lo_halo, send_sem=hsend.at[0],
            recv_sem=hrecv.at[0], device_id=(me, g + 1), device_id_type=MESH)

    def to_lo():
        return pltpu.make_async_remote_copy(
            src_ref=traces.at[pl.ds(0, ROWS)], dst_ref=hi_halo, send_sem=hsend.at[1],
            recv_sem=hrecv.at[1], device_id=(me, g - 1), device_id_type=MESH)

    @pl.when(has_hi)
    def _():
        to_hi().start()

    @pl.when(has_lo)
    def _():
        to_lo().start()

    def send(d):
        return pltpu.make_async_remote_copy(
            src_ref=ga.at[d], dst_ref=r.at[me + 1], send_sem=send_sem.at[d],
            recv_sem=recv_sem.at[me], device_id=(d, g), device_id_type=MESH)

    def target(k, e):
        flip = (me // 2 % 2 + 1 + e // 2) % 2
        return (own + columns - k) % columns * 4 + flip * 2 + e % 2

    early = columns // 2

    @pl.loop(0, early * 4)
    def _(i):
        d = target(i // 4, i % 4)

        @pl.when(jnp.logical_and(d != me, jnp.logical_and(d != 0, d != slabs - 1)))
        def _():
            send(d).start()

    @pl.when(has_lo)
    def _():
        to_hi().wait_recv()

    @pl.when(jnp.logical_not(has_lo))
    def _():
        lo_halo[...] = jnp.zeros_like(lo_halo)

    @pl.when(has_hi)
    def _():
        to_lo().wait_recv()

    @pl.when(jnp.logical_not(has_hi))
    def _():
        hi_halo[...] = jnp.zeros_like(hi_halo)

    edge = LANES - ROWS
    m = gauge_matrix(half_column(0)[:ROWS], LANES, ROWS)
    ga[0] = dot(m, stack(lo_halo[...], x[0:edge, :])).astype(BF16)
    m = gauge_matrix(half_column(chans // block - 1)[block - ROWS :], LANES, edge - ROWS)
    ga[slabs - 1] = dot(m, stack(x[chans - edge :, :], hi_halo[...])).astype(BF16)

    @pl.loop(0, columns * 4)
    def _(i):
        d = target(i // 4, i % 4)
        edge_row = jnp.logical_or(d == 0, d == slabs - 1)

        @pl.when(jnp.logical_and(d != me, jnp.logical_or(i >= early * 4, edge_row)))
        def _():
            send(d).start()

    r[pl.ds(me + 1, 1)] = ga[pl.ds(me, 1)]
    r[0] = jnp.zeros(r.shape[1:], BF16)
    r[slabs + 1] = jnp.zeros(r.shape[1:], BF16)
    for load in loads[2:]:
        load.wait()
    row = jnp.broadcast_to(taps[...], (FRAME, 2 * FRAME))
    toep[...] = pltpu.roll(row, 0, 1, stride=1, stride_axis=0).T.astype(BF16)
    earlier = iota((FRAME, 2 * FRAME), 0)
    sample = iota((FRAME, 2 * FRAME), 1)
    tile = sample // LANES % 2 == earlier // LANES
    through = earlier % LANES <= sample % LANES
    upto = jnp.where(jnp.logical_and(tile, through), 1.0, 0.0)
    after = jnp.where(jnp.logical_and(tile, jnp.logical_not(through)), -1.0, 0.0)
    both = jnp.where(sample < FRAME, upto, after).astype(BF16)
    for i in range(3):
        sums[i * FRAME : (i + 1) * FRAME] = both
    bins = iota((LANES, LANES), 0)
    band = iota((LANES, LANES), 1)
    select = jnp.zeros((LANES, LANES), F32)
    width_of = jnp.ones((NBANDS, LANES), F32)
    for b in range(NBANDS):
        low, high = edges[b], edges[b + 1]
        inside = jnp.logical_and(band == b, jnp.logical_and(bins >= low, bins < high))
        select = jnp.where(inside, 1.0, select)
        count = jnp.full((NBANDS, LANES), high - low, jnp.int32).astype(F32)
        width_of = jnp.where(iota((NBANDS, LANES), 0) == b, count, width_of)
    for i in range(2):
        sel[i * LANES : (i + 1) * LANES] = select.astype(BF16)
    widths[...] = width_of
    place = iota((ROWS, LANES), 0)
    for i, lengths in enumerate((sta, lta)):
        length = jnp.zeros((ROWS, LANES), jnp.int32)
        for c in range(ROWS):
            length = jnp.where(place == c, lengths[me * ROWS + c], length)
        turn[i] = length
        scale[i] = 1.0 / length.astype(F32)

    def receive(chunk):
        @pl.loop(0, STEP)
        def _(n):
            s = chunk * STEP + n

            @pl.when(s != me)
            def _():
                pltpu.make_async_remote_copy(
                    src_ref=ga.at[s], dst_ref=r.at[s + 1], send_sem=send_sem.at[s],
                    recv_sem=recv_sem.at[s], device_id=(s, g), device_id_type=MESH).wait_recv()

    rows = STEP * ROWS

    def compute(chunk):
        s0 = chunk * STEP

        def part(slab, q):
            return r[pl.ds(s0 + slab, STEP), :, q * LANES : (q + 1) * LANES].reshape(rows, LANES)

        mine = [part(1, q) for q in range(4)]
        ahead = r[pl.ds(s0, 1), :, LANES:].reshape(ROWS, 3 * LANES)
        windows = stack(
            lanes(ahead, mine[0][:ROWS]),
            lanes(part(0, 3), *mine[:3]),
            lanes(*mine[1:], part(2, 0)),
        )
        filtered = dot(windows, toep[...])
        high, low = split(filtered[ROWS:], 2)
        spectrum = dot(lanes(high, low, high), table[...])
        power = spectrum[:, :LANES] * spectrum[:, :LANES] + spectrum[:, LANES:] * spectrum[:, LANES:]
        total = dot(lanes(*split(power, 2)), sel[...])
        for n in range(STEP):
            for f in range(2):
                at = pl.multiple_of(((s0 + n) * 2 + f) * ROWS, ROWS)
                begin = f * rows + n * ROWS
                bands[pl.ds(at, ROWS), :] = total[begin : begin + ROWS]
        energy = filtered * filtered
        started = jnp.where(s0 > 0, 1.0, 0.0)
        energy = stack(energy[:ROWS] * started, energy[ROWS:])
        running = dot(lanes(*split(energy, 3)), sums[...])
        back = running[:ROWS, 3 * LANES :]
        first, second = running[ROWS : ROWS + rows], running[ROWS + rows :]
        ups = [first[:, :LANES], first[:, LANES:FRAME], second[:, :LANES], second[:, LANES:FRAME]]
        downs = [first[:, FRAME : 3 * LANES], first[:, 3 * LANES :], second[:, FRAME : 3 * LANES], second[:, 3 * LANES :]]
        downs = [stack(back, downs[3][: rows - ROWS])] + downs[:3]
        lane = iota((rows, LANES), 1)
        means = []
        for i in range(2):
            length = stack(*[turn[i]] * STEP)
            inverse = stack(*[scale[i]] * STEP)
            kept = lane < LANES - length
            source = (lane + (LANES - length)) % LANES
            means.append([
                (up - jnp.take_along_axis(jnp.where(kept, up, down), source, axis=1)) * inverse
                for up, down in zip(ups, downs)
            ])
        for q in range(4):
            ratio = (means[0][q] / jnp.maximum(means[1][q], 0.5)).astype(BF16)
            for n in range(STEP):
                at = pl.multiple_of((s0 + n) * 4 * LANES + q * LANES, LANES)
                ratio_out[:, pl.ds(at, LANES)] = ratio[n * ROWS : (n + 1) * ROWS]

    chunks = slabs // STEP
    begin = (own * 4 + STEP - 4) // STEP
    receive(begin % chunks)
    receive((begin + 1) % chunks)

    @pl.loop(1, chunks - 1)
    def _(i):
        receive((begin + i + 1) % chunks)
        compute((begin + i) % chunks)

    @pl.loop(chunks - 1, chunks + 1)
    def _(i):
        compute((begin + i) % chunks)

    frames = 2 * slabs

    @pl.loop(0, ROWS)
    def _(c):
        mean = bands[pl.ds(c, frames, stride=ROWS), :].T[:NBANDS] / widths[:, :frames]
        sig_out[c] = jnp.log1p(mean / FRAME)

    @pl.when(has_hi)
    def _():
        to_hi().wait_send()

    @pl.when(has_lo)
    def _():
        to_lo().wait_send()

    @pl.loop(1, slabs)
    def _(k):
        send((me + k) % slabs).wait_send()


def body(traces, fir_taps, gauge_half, sta_length, lta_length, band_edges):
    slabs, groups = lax.axis_size("tm"), lax.axis_size("grp")
    chans, local = traces.shape
    taps = jnp.pad(fir_taps.astype(F32), (REACH, 2 * FRAME - REACH - NTAPS))[None, :]
    half = gauge_half.reshape(-1, LANES)
    table = jnp.asarray(spectral_table())
    total = slabs * local
    vmem = pl.BlockSpec(memory_space=pltpu.VMEM)
    hbm = pl.BlockSpec(memory_space=pltpu.HBM)
    dma = pltpu.SemaphoreType.DMA
    ratio, signature = pl.pallas_call(
        functools.partial(kernel, slabs, groups),
        out_shape=(
            jax.ShapeDtypeStruct((ROWS, total), BF16),
            jax.ShapeDtypeStruct((ROWS, NBANDS, total // FRAME), F32),
        ),
        in_specs=[hbm] * 7,
        out_specs=(vmem, vmem),
        scratch_shapes=[
            pltpu.VMEM((chans, local), BF16),
            pltpu.VMEM((slabs, ROWS, local), BF16),
            pltpu.VMEM((slabs + 2, ROWS, local), BF16),
            pltpu.VMEM((ROWS, local), BF16),
            pltpu.VMEM((ROWS, local), BF16),
            pltpu.VMEM(taps.shape, taps.dtype),
            pltpu.VMEM(half.shape, half.dtype),
            pltpu.VMEM(table.shape, BF16),
            pltpu.VMEM((2 * FRAME, FRAME), BF16),
            pltpu.VMEM((3 * FRAME, 2 * FRAME), BF16),
            pltpu.VMEM((2 * LANES, LANES), BF16),
            pltpu.VMEM((NBANDS, LANES), F32),
            pltpu.VMEM((2, ROWS, LANES), jnp.int32),
            pltpu.VMEM((2, ROWS, LANES), F32),
            pltpu.VMEM((2 * slabs * ROWS, LANES), F32),
            pltpu.SMEM(sta_length.shape, jnp.int32),
            pltpu.SMEM(lta_length.shape, jnp.int32),
            pltpu.SMEM(band_edges.shape, jnp.int32),
            dma((7,)),
            dma((slabs,)),
            dma((slabs,)),
            dma((2,)),
            dma((2,)),
        ],
        compiler_params=pltpu.CompilerParams(
            collective_id=0, has_side_effects=True, vmem_limit_bytes=62 * 2**20
        ),
        cost_estimate=pl.CostEstimate(flops=4 * 10**9, bytes_accessed=3 * 2**20, transcendentals=0),
    )(traces, taps, half, sta_length, lta_length, band_edges, table)
    return ratio[None], signature[None]


def solution(mesh):
    in_specs = (P("grp", "tm"), P(), P("grp"), P("grp"), P("grp"), P())
    out_specs = (P("grp", "tm", None), P("grp", "tm", None, None))
    return jax.shard_map(body, mesh=mesh, in_specs=in_specs, out_specs=out_specs, check_vma=False)
```

```python
import functools
import math

import jax
import jax.numpy as jnp
import numpy as np
from jax import lax
from jax.experimental import pallas as pl
from jax.experimental.pallas import tpu as pltpu
from jax.sharding import PartitionSpec as P

NTAPS = 129
REACH = 64
LANES = 128
FRAME = 256
NBANDS = 8
ROWS = 16
STEP = 8
MESH = pl.DeviceIdType.MESH
F32 = jnp.float32
BF16 = jnp.bfloat16


def spectral_table():
    n = np.arange(FRAME)
    k = np.arange(FRAME // 2)
    angle = 2.0 * math.pi * ((n[:, None] * k[None, :]) % FRAME) / FRAME
    hann = 0.5 - 0.5 * np.cos(2.0 * math.pi * n / FRAME)
    table = np.concatenate([np.cos(angle), np.sin(angle)], axis=1) * hann[:, None]
    high = table.astype(jnp.bfloat16)
    low = (table - high.astype(np.float64)).astype(jnp.bfloat16)
    return np.concatenate([high, high, low], axis=0)


def iota(shape, dim):
    return lax.broadcasted_iota(jnp.int32, shape, dim)


def split(x, terms):
    parts = []
    for _ in range(terms - 1):
        parts.append(x.astype(BF16))
        x = x - parts[-1].astype(F32)
    return parts + [x.astype(BF16)]


def dot(a, b):
    return jnp.dot(a, b, preferred_element_type=F32)


def lanes(*parts):
    return jnp.concatenate(parts, axis=1)


def stack(*parts):
    return jnp.concatenate(parts, axis=0)


def gauge_matrix(half, width, off):
    n = half.shape[0]
    if width > LANES:
        half = lanes(*[half] * (width // LANES))
    rel = (iota((n, width), 1) - iota((n, width), 0) - off).astype(F32)
    side = jnp.where(jnp.abs(rel) == half, -0.5, 0.0)
    return jnp.where(rel == 0.0, 1.0, side).astype(BF16)


def wrap(i, n):
    return jnp.where(i >= n, i - n, i)


def finish(ratio, bands, widths, ratio_out, sig_out, sig, sems):
    whole = pltpu.make_async_copy(ratio, ratio_out.at[0], sems.at[0])
    whole.start()
    for c in range(ROWS):
        mean = bands[pl.ds(c, sig.shape[2], stride=ROWS), :].T[:NBANDS] / widths[:, : sig.shape[2]]
        sig[c] = jnp.log1p(mean / FRAME)
    logs = pltpu.make_async_copy(sig, sig_out.at[0], sems.at[1])
    logs.start()
    whole.wait()
    logs.wait()


def kernel(
    slabs, groups,
    traces, taps_in, half_in, sta_in, lta_in, edges_in, table_in,
    ratio_out, bands, widths,
    x, ga, r, lo_halo, hi_halo, taps, half, table, toep, sums, sel, turn, shorter, scale,
    sta, lta, edges,
    in_sem, send_sem, recv_sem, hsend, hrecv,
):
    me = lax.axis_index("tm")
    g = lax.axis_index("grp")
    chans = x.shape[0]
    block = LANES
    per = block // ROWS
    columns = slabs // 4
    own = me // 4
    has_lo = g > 0
    has_hi = g < groups - 1

    pairs = [(traces, x), (half_in, half), (table_in, table), (taps_in, taps), (sta_in, sta), (lta_in, lta), (edges_in, edges)]
    loads = [pltpu.make_async_copy(a, b, in_sem.at[i]) for i, (a, b) in enumerate(pairs)]
    for load in loads:
        load.start()
    barrier = pltpu.get_barrier_semaphore()

    @pl.loop(1, slabs)
    def _(k):
        pl.semaphore_signal(barrier, inc=1, device_id=(wrap(me + k, slabs), g), device_id_type=MESH)

    @pl.when(has_lo)
    def _():
        pl.semaphore_signal(barrier, inc=1, device_id=(me, g - 1), device_id_type=MESH)

    @pl.when(has_hi)
    def _():
        pl.semaphore_signal(barrier, inc=1, device_id=(me, g + 1), device_id_type=MESH)

    def half_column(i):
        row = jnp.broadcast_to(half[pl.ds(i, 1), :].astype(F32), (LANES, LANES))
        return row.T

    loads[0].wait()
    loads[1].wait()
    width = min(2 * LANES, chans)

    @pl.loop(0, chans // block)
    def _(i):
        start = jnp.clip(i * block - REACH, 0, chans - width)
        rows = x[pl.ds(pl.multiple_of(start, ROWS), width), :]
        m = gauge_matrix(half_column(i), width, i * block - start)
        ga[pl.ds(i * per, per)] = dot(m, rows).astype(BF16).reshape(per, ROWS, x.shape[1])

    neighbours = jnp.where(has_lo, 1, 0) + jnp.where(has_hi, 1, 0)
    pl.semaphore_wait(barrier, slabs - 1 + neighbours)

    def to_hi():
        return pltpu.make_async_remote_copy(
            src_ref=traces.at[pl.ds(chans - ROWS, ROWS)], dst_ref=lo_halo, send_sem=hsend.at[0],
            recv_sem=hrecv.at[0], device_id=(me, g + 1), device_id_type=MESH)

    def to_lo():
        return pltpu.make_async_remote_copy(
            src_ref=traces.at[pl.ds(0, ROWS)], dst_ref=hi_halo, send_sem=hsend.at[1],
            recv_sem=hrecv.at[1], device_id=(me, g - 1), device_id_type=MESH)

    @pl.when(has_hi)
    def _():
        to_hi().start()

    @pl.when(has_lo)
    def _():
        to_lo().start()

    def send(d):
        return pltpu.make_async_remote_copy(
            src_ref=ga.at[d], dst_ref=r.at[me + 1], send_sem=send_sem.at[d],
            recv_sem=recv_sem.at[me], device_id=(d, g), device_id_type=MESH)

    across = (own * 2 + 1 - me // 2 % 2) * 2
    beside = (own * 2 + me // 2 % 2) * 2

    def send_column(k, allowed):
        shift = jnp.where(k > own, columns - k, -k) * 4
        for e in range(4):
            d = (across if e < 2 else beside) + shift + e % 2

            @pl.when(allowed(d))
            def _():
                send(d).start()

    def on_edge(d):
        return jnp.logical_or(d == 0, d == slabs - 1)

    early = columns // 2

    @pl.loop(0, early)
    def _(k):
        send_column(k, lambda d: jnp.logical_and(d != me, jnp.logical_not(on_edge(d))))

    @pl.when(has_lo)
    def _():
        to_hi().wait_recv()

    @pl.when(jnp.logical_not(has_lo))
    def _():
        lo_halo[...] = jnp.zeros_like(lo_halo)

    @pl.when(has_hi)
    def _():
        to_lo().wait_recv()

    @pl.when(jnp.logical_not(has_hi))
    def _():
        hi_halo[...] = jnp.zeros_like(hi_halo)

    edge = LANES - ROWS
    m = gauge_matrix(half_column(0)[:ROWS], LANES, ROWS)
    ga[0] = dot(m, stack(lo_halo[...], x[0:edge, :])).astype(BF16)
    m = gauge_matrix(half_column(chans // block - 1)[block - ROWS :], LANES, edge - ROWS)
    ga[slabs - 1] = dot(m, stack(x[chans - edge :, :], hi_halo[...])).astype(BF16)

    for d in (0, slabs - 1):
        back = wrap(own + columns - d // 4, columns)

        @pl.when(jnp.logical_and(d != me, back < early))
        def _():
            send(d).start()

    @pl.loop(early, columns)
    def _(k):
        send_column(k, lambda d: d != me)

    r[pl.ds(me + 1, 1)] = ga[pl.ds(me, 1)]
    r[0] = jnp.zeros(r.shape[1:], BF16)
    r[slabs + 1] = jnp.zeros(r.shape[1:], BF16)
    for load in loads[2:]:
        load.wait()
    tap = taps[...].astype(F32).reshape(1, NTAPS)
    row = jnp.concatenate([tap, jnp.zeros((1, 2 * FRAME - NTAPS), F32)], axis=1)
    row = jnp.broadcast_to(row, (FRAME, 2 * FRAME))
    toep[...] = pltpu.roll(row, REACH, 1, stride=1, stride_axis=0).T.astype(BF16)
    earlier = iota((FRAME, FRAME), 0)
    sample = iota((FRAME, FRAME), 1)
    tile = sample // LANES == earlier // LANES
    upto = jnp.where(jnp.logical_and(tile, earlier <= sample), 1.0, 0.0).astype(BF16)
    for i in range(3):
        sums[i * FRAME : (i + 1) * FRAME] = upto
    bins = iota((LANES, LANES), 0)
    band = iota((LANES, LANES), 1)
    select = jnp.zeros((LANES, LANES), F32)
    width_of = jnp.ones((NBANDS, LANES), F32)
    for b in range(NBANDS):
        low, high = edges[b], edges[b + 1]
        inside = jnp.logical_and(band == b, jnp.logical_and(bins >= low, bins < high))
        select = jnp.where(inside, 1.0, select)
        count = jnp.full((NBANDS, LANES), high - low, jnp.int32).astype(F32)
        width_of = jnp.where(iota((NBANDS, LANES), 0) == b, count, width_of)
    for i in range(2):
        sel[i * LANES : (i + 1) * LANES] = select.astype(BF16)
    widths[...] = width_of
    place = iota((ROWS, LANES), 0)
    for i, lengths in enumerate((sta, lta)):
        length = jnp.zeros((ROWS, LANES), jnp.int32)
        for c in range(ROWS):
            length = jnp.where(place == c, lengths[me * ROWS + c], length)
        source = iota((ROWS, LANES), 1) - length
        turn[i] = jnp.where(source < 0, source + LANES, source)
        shorter[i] = LANES - length
        scale[i] = 1.0 / length.astype(F32)

    def receive(chunk):
        @pl.loop(0, STEP)
        def _(n):
            s = chunk * STEP + n

            @pl.when(s != me)
            def _():
                pltpu.make_async_remote_copy(
                    src_ref=ga.at[s], dst_ref=r.at[s + 1], send_sem=send_sem.at[s],
                    recv_sem=recv_sem.at[s], device_id=(s, g), device_id_type=MESH).wait_recv()

    rows = STEP * ROWS

    def compute(chunk):
        s0 = chunk * STEP

        def part(slab, q):
            return r[pl.ds(s0 + slab, STEP), :, q * LANES : (q + 1) * LANES].reshape(rows, LANES)

        mine = [part(1, q) for q in range(4)]
        ahead = r[pl.ds(s0, 1), :, LANES:].reshape(ROWS, 3 * LANES)
        windows = stack(
            lanes(ahead, mine[0][:ROWS]),
            lanes(part(0, 3), *mine[:3]),
            lanes(*mine[1:], part(2, 0)),
        )
        filtered = dot(windows, toep[...])
        high, low = split(filtered[ROWS:], 2)
        spectrum = dot(lanes(high, low, high), table[...])
        power = spectrum[:, :LANES] * spectrum[:, :LANES] + spectrum[:, LANES:] * spectrum[:, LANES:]
        total = dot(lanes(*split(power, 2)), sel[...])
        for n in range(STEP):
            for f in range(2):
                at = pl.multiple_of(((s0 + n) * 2 + f) * ROWS, ROWS)
                begin = f * rows + n * ROWS
                bands[pl.ds(at, ROWS), :] = total[begin : begin + ROWS]
        energy = filtered * filtered
        started = jnp.where(s0 > 0, 1.0, 0.0)
        energy = stack(energy[:ROWS] * started, energy[ROWS:])
        running = dot(lanes(*split(energy, 3)), sums[...])
        back = running[:ROWS, LANES:]
        first, second = running[ROWS : ROWS + rows], running[ROWS + rows :]
        ups = [first[:, :LANES], first[:, LANES:], second[:, :LANES], second[:, LANES:]]
        downs = [stack(back, ups[3][: rows - ROWS])] + ups[:3]
        downs = [down - down[:, LANES - 1 :] for down in downs]
        lane = iota((rows, LANES), 1)
        means = []
        for i in range(2):
            kept = lane < stack(*[shorter[i]] * STEP)
            inverse = stack(*[scale[i]] * STEP)
            source = stack(*[turn[i]] * STEP)
            means.append([
                (up - jnp.take_along_axis(jnp.where(kept, up, down), source, axis=1)) * inverse
                for up, down in zip(ups, downs)
            ])
        for q in range(4):
            ratio = (means[0][q] / jnp.maximum(means[1][q], 0.5)).astype(BF16)
            for n in range(STEP):
                at = pl.multiple_of((s0 + n) * 4 * LANES + q * LANES, LANES)
                ratio_out[:, pl.ds(at, LANES)] = ratio[n * ROWS : (n + 1) * ROWS]

    chunks = slabs // STEP
    begin = (own * 4 + STEP - 4) // STEP
    receive(begin % chunks)
    receive((begin + 1) % chunks)

    @pl.loop(1, chunks - 1)
    def _(i):
        receive((begin + i + 1) % chunks)
        compute((begin + i) % chunks)

    @pl.loop(chunks - 1, chunks + 1)
    def _(i):
        compute((begin + i) % chunks)

    @pl.when(has_hi)
    def _():
        to_hi().wait_send()

    @pl.when(has_lo)
    def _():
        to_lo().wait_send()

    @pl.loop(1, slabs)
    def _(k):
        send(wrap(me + k, slabs)).wait_send()


def body(traces, fir_taps, gauge_half, sta_length, lta_length, band_edges):
    slabs, groups = lax.axis_size("tm"), lax.axis_size("grp")
    chans, local = traces.shape
    taps = fir_taps
    half = gauge_half.reshape(-1, LANES)
    table = jnp.asarray(spectral_table())
    total = slabs * local
    vmem = pl.BlockSpec(memory_space=pltpu.VMEM)
    hbm = pl.BlockSpec(memory_space=pltpu.HBM)
    dma = pltpu.SemaphoreType.DMA
    operands = (traces, taps, half, sta_length, lta_length, band_edges, table)
    operands = [pltpu.with_memory_space_constraint(a, pltpu.HBM) for a in operands]
    ratio, bands, widths = pl.pallas_call(
        functools.partial(kernel, slabs, groups),
        out_shape=(
            jax.ShapeDtypeStruct((ROWS, total), BF16),
            jax.ShapeDtypeStruct((total // FRAME * ROWS, LANES), F32),
            jax.ShapeDtypeStruct((NBANDS, LANES), F32),
        ),
        in_specs=[hbm] * 7,
        out_specs=(vmem, vmem, vmem),
        scratch_shapes=[
            pltpu.VMEM((chans, local), BF16),
            pltpu.VMEM((slabs, ROWS, local), BF16),
            pltpu.VMEM((slabs + 2, ROWS, local), BF16),
            pltpu.VMEM((ROWS, local), BF16),
            pltpu.VMEM((ROWS, local), BF16),
            pltpu.VMEM(taps.shape, taps.dtype),
            pltpu.VMEM(half.shape, half.dtype),
            pltpu.VMEM(table.shape, BF16),
            pltpu.VMEM((2 * FRAME, FRAME), BF16),
            pltpu.VMEM((3 * FRAME, FRAME), BF16),
            pltpu.VMEM((2 * LANES, LANES), BF16),
            pltpu.VMEM((2, ROWS, LANES), jnp.int32),
            pltpu.VMEM((2, ROWS, LANES), jnp.int32),
            pltpu.VMEM((2, ROWS, LANES), F32),
            pltpu.SMEM(sta_length.shape, jnp.int32),
            pltpu.SMEM(lta_length.shape, jnp.int32),
            pltpu.SMEM(band_edges.shape, jnp.int32),
            dma((7,)),
            dma((slabs,)),
            dma((slabs,)),
            dma((2,)),
            dma((2,)),
        ],
        compiler_params=pltpu.CompilerParams(
            collective_id=0, has_side_effects=True, vmem_limit_bytes=40 * 2**20
        ),
        cost_estimate=pl.CostEstimate(flops=4 * 10**9, bytes_accessed=3 * 2**20, transcendentals=0),
    )(*operands)
    frames = total // FRAME
    return pl.pallas_call(
        finish,
        out_shape=(
            jax.ShapeDtypeStruct((1, ROWS, total), BF16),
            jax.ShapeDtypeStruct((1, ROWS, NBANDS, frames), F32),
        ),
        in_specs=[vmem] * 3,
        out_specs=(hbm, hbm),
        scratch_shapes=[pltpu.VMEM((ROWS, NBANDS, frames), F32), dma((2,))],
        compiler_params=pltpu.CompilerParams(vmem_limit_bytes=8 * 2**20),
    )(ratio, bands, widths)


def solution(mesh):
    in_specs = (P("grp", "tm"), P(), P("grp"), P("grp"), P("grp"), P())
    out_specs = (P("grp", "tm", None), P("grp", "tm", None, None))
    return jax.shard_map(body, mesh=mesh, in_specs=in_specs, out_specs=out_specs, check_vma=False)
```

```python
import functools
import math

import jax
import jax.numpy as jnp
import numpy as np
from jax import lax
from jax.experimental import pallas as pl
from jax.experimental.pallas import tpu as pltpu
from jax.sharding import PartitionSpec as P

NTAPS = 129
REACH = 64
LANES = 128
FRAME = 256
NBANDS = 8
ROWS = 16
STEP = 8
MESH = pl.DeviceIdType.MESH
F32 = jnp.float32
BF16 = jnp.bfloat16


def spectral_table():
    n = np.arange(FRAME)
    k = np.arange(FRAME // 2)
    angle = 2.0 * math.pi * ((n[:, None] * k[None, :]) % FRAME) / FRAME
    hann = 0.5 - 0.5 * np.cos(2.0 * math.pi * n / FRAME)
    table = np.concatenate([np.cos(angle), np.sin(angle)], axis=1) * hann[:, None]
    high = table.astype(jnp.bfloat16)
    low = (table - high.astype(np.float64)).astype(jnp.bfloat16)
    return np.concatenate([high, high, low], axis=0)


def iota(shape, dim):
    return lax.broadcasted_iota(jnp.int32, shape, dim)


def split(x, terms):
    parts = []
    for _ in range(terms - 1):
        parts.append(x.astype(BF16))
        x = x - parts[-1].astype(F32)
    return parts + [x.astype(BF16)]


def dot(a, b):
    return jnp.dot(a, b, preferred_element_type=F32)


def lanes(*parts):
    return jnp.concatenate(parts, axis=1)


def stack(*parts):
    return jnp.concatenate(parts, axis=0)


def gauge_matrix(half, width, off):
    n = half.shape[0]
    if width > LANES:
        half = lanes(*[half] * (width // LANES))
    rel = (iota((n, width), 1) - iota((n, width), 0) - off).astype(F32)
    side = jnp.where(jnp.abs(rel) == half, -0.5, 0.0)
    return jnp.where(rel == 0.0, 1.0, side).astype(BF16)


def wrap(i, n):
    return jnp.where(i >= n, i - n, i)


def finish(ratio, bands, widths, ratio_out, sig_out, sig, sems):
    whole = pltpu.make_async_copy(ratio, ratio_out.at[0], sems.at[0])
    whole.start()
    for c in range(ROWS):
        mean = bands[pl.ds(c, sig.shape[2], stride=ROWS), :].T[:NBANDS] / widths[:, : sig.shape[2]]
        sig[c] = jnp.log1p(mean / FRAME)
    logs = pltpu.make_async_copy(sig, sig_out.at[0], sems.at[1])
    logs.start()
    whole.wait()
    logs.wait()


def kernel(
    slabs, groups,
    traces, taps_in, half_in, sta_in, lta_in, edges_in, table_in,
    ratio_out, bands, widths,
    x, ga, r, lo_halo, hi_halo, taps, half, table, toep, sums, sel, turn, shorter, scale,
    sta, lta, edges,
    in_sem, send_sem, recv_sem, hsend, hrecv,
):
    me = lax.axis_index("tm")
    g = lax.axis_index("grp")
    chans = x.shape[0]
    block = LANES
    per = block // ROWS
    columns = slabs // 4
    own = me // 4
    has_lo = g > 0
    has_hi = g < groups - 1

    barrier = pltpu.get_barrier_semaphore()

    @pl.loop(1, slabs, unroll=True)
    def _(k):
        pl.semaphore_signal(barrier, inc=1, device_id=(wrap(me + k, slabs), g), device_id_type=MESH)

    @pl.when(has_lo)
    def _():
        pl.semaphore_signal(barrier, inc=1, device_id=(me, g - 1), device_id_type=MESH)

    @pl.when(has_hi)
    def _():
        pl.semaphore_signal(barrier, inc=1, device_id=(me, g + 1), device_id_type=MESH)

    pairs = [(traces, x), (half_in, half), (table_in, table), (taps_in, taps), (sta_in, sta), (lta_in, lta), (edges_in, edges)]
    loads = [pltpu.make_async_copy(a, b, in_sem.at[i]) for i, (a, b) in enumerate(pairs)]
    for load in loads:
        load.start()
    def half_column(i):
        row = jnp.broadcast_to(half[pl.ds(i, 1), :].astype(F32), (LANES, LANES))
        return row.T

    loads[0].wait()
    loads[1].wait()
    width = min(2 * LANES, chans)

    @pl.loop(0, chans // block)
    def _(i):
        start = jnp.clip(i * block - REACH, 0, chans - width)
        rows = x[pl.ds(pl.multiple_of(start, ROWS), width), :]
        m = gauge_matrix(half_column(i), width, i * block - start)
        ga[pl.ds(i * per, per)] = dot(m, rows).astype(BF16).reshape(per, ROWS, x.shape[1])

    neighbours = jnp.where(has_lo, 1, 0) + jnp.where(has_hi, 1, 0)
    pl.semaphore_wait(barrier, slabs - 1 + neighbours)

    def to_hi():
        return pltpu.make_async_remote_copy(
            src_ref=traces.at[pl.ds(chans - ROWS, ROWS)], dst_ref=lo_halo, send_sem=hsend.at[0],
            recv_sem=hrecv.at[0], device_id=(me, g + 1), device_id_type=MESH)

    def to_lo():
        return pltpu.make_async_remote_copy(
            src_ref=traces.at[pl.ds(0, ROWS)], dst_ref=hi_halo, send_sem=hsend.at[1],
            recv_sem=hrecv.at[1], device_id=(me, g - 1), device_id_type=MESH)

    @pl.when(has_hi)
    def _():
        to_hi().start()

    @pl.when(has_lo)
    def _():
        to_lo().start()

    seat = me % 4

    def send(d, back):
        return pltpu.make_async_remote_copy(
            src_ref=ga.at[d], dst_ref=r.at[back * 4 + seat], send_sem=send_sem,
            recv_sem=recv_sem.at[back], device_id=(d, g), device_id_type=MESH)

    across = (own * 2 + 1 - me // 2 % 2) * 2
    beside = (own * 2 + me // 2 % 2) * 2

    def send_column(k, allowed):
        shift = jnp.where(k > own, columns - k, -k) * 4
        for e in range(4):
            d = (across if e < 2 else beside) + shift + e % 2

            @pl.when(allowed(d))
            def _():
                send(d, k).start()

    def on_edge(d):
        return jnp.logical_or(d == 0, d == slabs - 1)

    early = columns // 2

    @pl.loop(0, early)
    def _(k):
        send_column(k, lambda d: jnp.logical_and(d != me, jnp.logical_not(on_edge(d))))

    @pl.when(has_lo)
    def _():
        to_hi().wait_recv()

    @pl.when(jnp.logical_not(has_lo))
    def _():
        lo_halo[...] = jnp.zeros_like(lo_halo)

    @pl.when(has_hi)
    def _():
        to_lo().wait_recv()

    @pl.when(jnp.logical_not(has_hi))
    def _():
        hi_halo[...] = jnp.zeros_like(hi_halo)

    edge = LANES - ROWS
    m = gauge_matrix(half_column(0)[:ROWS], LANES, ROWS)
    ga[0] = dot(m, stack(lo_halo[...], x[0:edge, :])).astype(BF16)
    m = gauge_matrix(half_column(chans // block - 1)[block - ROWS :], LANES, edge - ROWS)
    ga[slabs - 1] = dot(m, stack(x[chans - edge :, :], hi_halo[...])).astype(BF16)

    for d in (0, slabs - 1):
        back = wrap(own + columns - d // 4, columns)

        @pl.when(jnp.logical_and(d != me, back < early))
        def _():
            send(d, back).start()

    @pl.loop(early, columns)
    def _(k):
        send_column(k, lambda d: d != me)

    r[pl.ds(seat, 1)] = ga[pl.ds(me, 1)]
    for load in loads[2:]:
        load.wait()
    tap = taps[...].astype(F32).reshape(1, NTAPS)
    row = jnp.concatenate([tap, jnp.zeros((1, 2 * FRAME - NTAPS), F32)], axis=1)
    row = jnp.broadcast_to(row, (FRAME, 2 * FRAME))
    toep[...] = pltpu.roll(row, REACH, 1, stride=1, stride_axis=0).T.astype(BF16)
    earlier = iota((FRAME, FRAME), 0)
    sample = iota((FRAME, FRAME), 1)
    tile = sample // LANES == earlier // LANES
    upto = jnp.where(jnp.logical_and(tile, earlier <= sample), 1.0, 0.0).astype(BF16)
    for i in range(3):
        sums[i * FRAME : (i + 1) * FRAME] = upto
    bins = iota((LANES, LANES), 0)
    band = iota((LANES, LANES), 1)
    select = jnp.zeros((LANES, LANES), F32)
    width_of = jnp.ones((NBANDS, LANES), F32)
    for b in range(NBANDS):
        low, high = edges[b], edges[b + 1]
        inside = jnp.logical_and(band == b, jnp.logical_and(bins >= low, bins < high))
        select = jnp.where(inside, 1.0, select)
        count = jnp.full((NBANDS, LANES), high - low, jnp.int32).astype(F32)
        width_of = jnp.where(iota((NBANDS, LANES), 0) == b, count, width_of)
    for i in range(2):
        sel[i * LANES : (i + 1) * LANES] = select.astype(BF16)
    widths[...] = width_of
    place = iota((ROWS, LANES), 0)
    for i, lengths in enumerate((sta, lta)):
        length = jnp.zeros((ROWS, LANES), jnp.int32)
        for c in range(ROWS):
            length = jnp.where(place == c, lengths[me * ROWS + c], length)
        source = iota((ROWS, LANES), 1) - length
        turn[i] = jnp.where(source < 0, source + LANES, source)
        shorter[i] = LANES - length
        scale[i] = 1.0 / length.astype(F32)

    def receive(column, count):
        pltpu.make_async_remote_copy(
            src_ref=ga.at[pl.ds(0, count)], dst_ref=r.at[pl.ds(column * 4, count)], send_sem=send_sem,
            recv_sem=recv_sem.at[column], device_id=(wrap(me + 1, slabs), g), device_id_type=MESH).wait_recv()

    rows = STEP * ROWS

    def compute(i):
        base = i * STEP
        first = (own * 4 + base + 1) % slabs
        place = [wrap(first + n, slabs) for n in range(STEP)]

        def part(o, q):
            return r[pl.ds(base + o, STEP), :, q * LANES : (q + 1) * LANES].reshape(rows, LANES)

        slab = iota((rows, LANES), 0) // ROWS
        follows = jnp.where(slab == wrap(slabs - first, slabs), 0.0, 1.0)
        goes_on = jnp.where(slab == slabs - 1 - first, 0.0, 1.0)
        mine = [part(1, q) for q in range(4)]
        ahead = r[pl.ds(base, 1), :, LANES:].reshape(ROWS, 3 * LANES)
        windows = stack(
            lanes(ahead, mine[0][:ROWS]),
            lanes(part(0, 3) * follows.astype(BF16), *mine[:3]),
            lanes(*mine[1:], part(2, 0) * goes_on.astype(BF16)),
        )
        filtered = dot(windows, toep[...])
        high, low = split(filtered[ROWS:], 2)
        spectrum = dot(lanes(high, low, high), table[...])
        power = spectrum[:, :LANES] * spectrum[:, :LANES] + spectrum[:, LANES:] * spectrum[:, LANES:]
        total = dot(lanes(*split(power, 2)), sel[...])
        for n in range(STEP):
            for f in range(2):
                at = pl.multiple_of((place[n] * 2 + f) * ROWS, ROWS)
                begin = f * rows + n * ROWS
                bands[pl.ds(at, ROWS), :] = total[begin : begin + ROWS]
        energy = filtered * filtered
        running = dot(lanes(*split(energy, 3)), sums[...])
        back = running[:ROWS, LANES:]
        left, right = running[ROWS : ROWS + rows], running[ROWS + rows :]
        ups = [left[:, :LANES], left[:, LANES:], right[:, :LANES], right[:, LANES:]]
        downs = [stack(back, ups[3][: rows - ROWS]) * follows] + ups[:3]
        downs = [down - down[:, LANES - 1 :] for down in downs]
        lane = iota((rows, LANES), 1)
        means = []
        for i in range(2):
            kept = lane < stack(*[shorter[i]] * STEP)
            inverse = stack(*[scale[i]] * STEP)
            source = stack(*[turn[i]] * STEP)
            means.append([
                (up - jnp.take_along_axis(jnp.where(kept, up, down), source, axis=1)) * inverse
                for up, down in zip(ups, downs)
            ])
        for q in range(4):
            ratio = (means[0][q] / jnp.maximum(means[1][q], 0.5)).astype(BF16)
            for n in range(STEP):
                at = pl.multiple_of(place[n] * 4 * LANES + q * LANES, LANES)
                ratio_out[:, pl.ds(at, LANES)] = ratio[n * ROWS : (n + 1) * ROWS]

    receive(0, 3)
    r[slabs] = r[0]
    r[slabs + 1] = r[1]

    @pl.loop(0, slabs // STEP)
    def _(i):
        for n in range(STEP // 4):
            column = i * (STEP // 4) + 1 + n

            @pl.when(column < columns)
            def _():
                receive(column, 4)

        compute(i)

    @pl.when(has_hi)
    def _():
        to_hi().wait_send()

    @pl.when(has_lo)
    def _():
        to_lo().wait_send()

    pltpu.make_async_remote_copy(
        src_ref=ga.at[pl.ds(0, slabs - 1)], dst_ref=r.at[pl.ds(0, slabs - 1)], send_sem=send_sem,
        recv_sem=recv_sem.at[0], device_id=(wrap(me + 1, slabs), g), device_id_type=MESH).wait_send()


def body(traces, fir_taps, gauge_half, sta_length, lta_length, band_edges):
    slabs, groups = lax.axis_size("tm"), lax.axis_size("grp")
    chans, local = traces.shape
    taps = fir_taps
    half = gauge_half.reshape(-1, LANES)
    table = jnp.asarray(spectral_table())
    total = slabs * local
    vmem = pl.BlockSpec(memory_space=pltpu.VMEM)
    hbm = pl.BlockSpec(memory_space=pltpu.HBM)
    dma = pltpu.SemaphoreType.DMA
    operands = (traces, taps, half, sta_length, lta_length, band_edges, table)
    operands = [pltpu.with_memory_space_constraint(a, pltpu.HBM) for a in operands]
    ratio, bands, widths = pl.pallas_call(
        functools.partial(kernel, slabs, groups),
        out_shape=(
            jax.ShapeDtypeStruct((ROWS, total), BF16),
            jax.ShapeDtypeStruct((total // FRAME * ROWS, LANES), F32),
            jax.ShapeDtypeStruct((NBANDS, LANES), F32),
        ),
        in_specs=[hbm] * 7,
        out_specs=(vmem, vmem, vmem),
        scratch_shapes=[
            pltpu.VMEM((chans, local), BF16),
            pltpu.VMEM((slabs, ROWS, local), BF16),
            pltpu.VMEM((slabs + 2, ROWS, local), BF16),
            pltpu.VMEM((ROWS, local), BF16),
            pltpu.VMEM((ROWS, local), BF16),
            pltpu.VMEM(taps.shape, taps.dtype),
            pltpu.VMEM(half.shape, half.dtype),
            pltpu.VMEM(table.shape, BF16),
            pltpu.VMEM((2 * FRAME, FRAME), BF16),
            pltpu.VMEM((3 * FRAME, FRAME), BF16),
            pltpu.VMEM((2 * LANES, LANES), BF16),
            pltpu.VMEM((2, ROWS, LANES), jnp.int32),
            pltpu.VMEM((2, ROWS, LANES), jnp.int32),
            pltpu.VMEM((2, ROWS, LANES), F32),
            pltpu.SMEM(sta_length.shape, jnp.int32),
            pltpu.SMEM(lta_length.shape, jnp.int32),
            pltpu.SMEM(band_edges.shape, jnp.int32),
            dma((7,)),
            dma,
            dma((slabs // 4,)),
            dma((2,)),
            dma((2,)),
        ],
        compiler_params=pltpu.CompilerParams(
            collective_id=0, has_side_effects=True, vmem_limit_bytes=40 * 2**20
        ),
        cost_estimate=pl.CostEstimate(flops=4 * 10**9, bytes_accessed=3 * 2**20, transcendentals=0),
    )(*operands)
    frames = total // FRAME
    return pl.pallas_call(
        finish,
        out_shape=(
            jax.ShapeDtypeStruct((1, ROWS, total), BF16),
            jax.ShapeDtypeStruct((1, ROWS, NBANDS, frames), F32),
        ),
        in_specs=[vmem] * 3,
        out_specs=(hbm, hbm),
        scratch_shapes=[pltpu.VMEM((ROWS, NBANDS, frames), F32), dma((2,))],
        compiler_params=pltpu.CompilerParams(vmem_limit_bytes=8 * 2**20),
    )(ratio, bands, widths)


def solution(mesh):
    in_specs = (P("grp", "tm"), P(), P("grp"), P("grp"), P("grp"), P())
    out_specs = (P("grp", "tm", None), P("grp", "tm", None, None))
    return jax.shard_map(body, mesh=mesh, in_specs=in_specs, out_specs=out_specs, check_vma=False)
```

```python
import functools
import math

import jax
import jax.numpy as jnp
import numpy as np
from jax import lax
from jax.experimental import pallas as pl
from jax.experimental.pallas import tpu as pltpu
from jax.sharding import PartitionSpec as P

NTAPS = 129
REACH = 64
LANES = 128
FRAME = 256
NBANDS = 8
ROWS = 16
STEP = 16
MESH = pl.DeviceIdType.MESH
F32 = jnp.float32
BF16 = jnp.bfloat16


def spectral_table():
    n = np.arange(FRAME)
    k = np.arange(FRAME // 2)
    angle = 2.0 * math.pi * ((n[:, None] * k[None, :]) % FRAME) / FRAME
    hann = 0.5 - 0.5 * np.cos(2.0 * math.pi * n / FRAME)
    table = np.concatenate([np.cos(angle), np.sin(angle)], axis=1) * hann[:, None]
    high = table.astype(jnp.bfloat16)
    low = (table - high.astype(np.float64)).astype(jnp.bfloat16)
    return np.concatenate([high, high, low], axis=0)


def iota(shape, dim):
    return lax.broadcasted_iota(jnp.int32, shape, dim)


def split(x, terms):
    parts = []
    for _ in range(terms - 1):
        parts.append(x.astype(BF16))
        x = x - parts[-1].astype(F32)
    return parts + [x.astype(BF16)]


def dot(a, b):
    return jnp.dot(a, b, preferred_element_type=F32)


def lanes(*parts):
    return jnp.concatenate(parts, axis=1)


def stack(*parts):
    return jnp.concatenate(parts, axis=0)


def gauge_matrix(half, width, off):
    n = half.shape[0]
    if width > LANES:
        half = lanes(*[half] * (width // LANES))
    rel = (iota((n, width), 1) - iota((n, width), 0) - off).astype(F32)
    side = jnp.where(jnp.abs(rel) == half, -0.5, 0.0)
    return jnp.where(rel == 0.0, 1.0, side).astype(BF16)


def wrap(i, n):
    return jnp.where(i >= n, i - n, i)


def finish(ratio, bands, widths, ratio_out, sig_out, sig, sems):
    whole = pltpu.make_async_copy(ratio, ratio_out.at[0], sems.at[0])
    whole.start()
    for c in range(ROWS):
        mean = bands[pl.ds(c, sig.shape[2], stride=ROWS), :].T[:NBANDS] / widths[:, : sig.shape[2]]
        sig[c] = jnp.log1p(mean / FRAME)
    logs = pltpu.make_async_copy(sig, sig_out.at[0], sems.at[1])
    logs.start()
    whole.wait()
    logs.wait()


def kernel(
    slabs, groups,
    traces, taps_in, half_in, sta_in, lta_in, edges_in, table_in,
    ratio_out, bands, widths,
    x, ga, r, lo_halo, hi_halo, taps, half, table, toep, sums, sel, turn, shorter, scale,
    sta, lta, edges,
    in_sem, send_sem, recv_sem, hsend, hrecv,
):
    me = lax.axis_index("tm")
    g = lax.axis_index("grp")
    chans = x.shape[0]
    block = LANES
    per = block // ROWS
    columns = slabs // 4
    own = me // 4
    has_lo = g > 0
    has_hi = g < groups - 1

    barrier = pltpu.get_barrier_semaphore()

    @pl.loop(1, slabs, unroll=True)
    def _(k):
        pl.semaphore_signal(barrier, inc=1, device_id=(wrap(me + k, slabs), g), device_id_type=MESH)

    @pl.when(has_lo)
    def _():
        pl.semaphore_signal(barrier, inc=1, device_id=(me, g - 1), device_id_type=MESH)

    @pl.when(has_hi)
    def _():
        pl.semaphore_signal(barrier, inc=1, device_id=(me, g + 1), device_id_type=MESH)

    pairs = [(traces, x), (half_in, half), (table_in, table), (taps_in, taps), (sta_in, sta), (lta_in, lta), (edges_in, edges)]
    loads = [pltpu.make_async_copy(a, b, in_sem.at[i]) for i, (a, b) in enumerate(pairs)]
    for load in loads:
        load.start()
    def half_column(i):
        row = jnp.broadcast_to(half[pl.ds(i, 1), :].astype(F32), (LANES, LANES))
        return row.T

    loads[0].wait()
    loads[1].wait()
    width = min(2 * LANES, chans)

    @pl.loop(0, chans // block, unroll=4)
    def _(i):
        start = jnp.clip(i * block - REACH, 0, chans - width)
        rows = x[pl.ds(pl.multiple_of(start, ROWS), width), :]
        m = gauge_matrix(half_column(i), width, i * block - start)
        ga[pl.ds(i * per, per)] = dot(m, rows).astype(BF16).reshape(per, ROWS, x.shape[1])

    neighbours = jnp.where(has_lo, 1, 0) + jnp.where(has_hi, 1, 0)
    pl.semaphore_wait(barrier, slabs - 1 + neighbours)

    def to_hi():
        return pltpu.make_async_remote_copy(
            src_ref=traces.at[pl.ds(chans - ROWS, ROWS)], dst_ref=lo_halo, send_sem=hsend.at[0],
            recv_sem=hrecv.at[0], device_id=(me, g + 1), device_id_type=MESH)

    def to_lo():
        return pltpu.make_async_remote_copy(
            src_ref=traces.at[pl.ds(0, ROWS)], dst_ref=hi_halo, send_sem=hsend.at[1],
            recv_sem=hrecv.at[1], device_id=(me, g - 1), device_id_type=MESH)

    @pl.when(has_hi)
    def _():
        to_hi().start()

    @pl.when(has_lo)
    def _():
        to_lo().start()

    seat = me % 4

    def send(d, back):
        return pltpu.make_async_remote_copy(
            src_ref=ga.at[d], dst_ref=r.at[back * 4 + seat], send_sem=send_sem,
            recv_sem=recv_sem.at[back], device_id=(d, g), device_id_type=MESH)

    across = (own * 2 + 1 - me // 2 % 2) * 2
    beside = (own * 2 + me // 2 % 2) * 2

    def send_column(k, allowed):
        shift = jnp.where(k > own, columns - k, -k) * 4
        for e in range(4):
            d = (across if e < 2 else beside) + shift + e % 2

            @pl.when(allowed(d))
            def _():
                send(d, k).start()

    def on_edge(d):
        return jnp.logical_or(d == 0, d == slabs - 1)

    early = columns // 2

    @pl.loop(0, early)
    def _(k):
        send_column(k, lambda d: jnp.logical_and(d != me, jnp.logical_not(on_edge(d))))

    @pl.when(has_lo)
    def _():
        to_hi().wait_recv()

    @pl.when(jnp.logical_not(has_lo))
    def _():
        lo_halo[...] = jnp.zeros_like(lo_halo)

    @pl.when(has_hi)
    def _():
        to_lo().wait_recv()

    @pl.when(jnp.logical_not(has_hi))
    def _():
        hi_halo[...] = jnp.zeros_like(hi_halo)

    edge = LANES - ROWS
    m = gauge_matrix(half_column(0)[:ROWS], LANES, ROWS)
    ga[0] = dot(m, stack(lo_halo[...], x[0:edge, :])).astype(BF16)
    m = gauge_matrix(half_column(chans // block - 1)[block - ROWS :], LANES, edge - ROWS)
    ga[slabs - 1] = dot(m, stack(x[chans - edge :, :], hi_halo[...])).astype(BF16)

    for d in (0, slabs - 1):
        back = wrap(own + columns - d // 4, columns)

        @pl.when(jnp.logical_and(d != me, back < early))
        def _():
            send(d, back).start()

    @pl.loop(early, columns)
    def _(k):
        send_column(k, lambda d: d != me)

    r[pl.ds(seat, 1)] = ga[pl.ds(me, 1)]
    for load in loads[2:]:
        load.wait()
    tap = taps[...].astype(F32).reshape(1, NTAPS)
    row = jnp.concatenate([tap, jnp.zeros((1, 2 * FRAME - NTAPS), F32)], axis=1)
    row = jnp.broadcast_to(row, (FRAME, 2 * FRAME))
    toep[...] = pltpu.roll(row, REACH, 1, stride=1, stride_axis=0).T.astype(BF16)
    earlier = iota((FRAME, FRAME), 0)
    sample = iota((FRAME, FRAME), 1)
    upto = jnp.where(earlier <= sample, 1.0, 0.0).astype(BF16)
    for i in range(3):
        sums[i * FRAME : (i + 1) * FRAME] = upto
    bins = iota((LANES, LANES), 0)
    band = iota((LANES, LANES), 1)
    select = jnp.zeros((LANES, LANES), F32)
    width_of = jnp.ones((NBANDS, LANES), F32)
    for b in range(NBANDS):
        low, high = edges[b], edges[b + 1]
        inside = jnp.logical_and(band == b, jnp.logical_and(bins >= low, bins < high))
        select = jnp.where(inside, 1.0, select)
        count = jnp.full((NBANDS, LANES), high - low, jnp.int32).astype(F32)
        width_of = jnp.where(iota((NBANDS, LANES), 0) == b, count, width_of)
    for i in range(2):
        sel[i * LANES : (i + 1) * LANES] = select.astype(BF16)
    widths[...] = width_of
    place = iota((ROWS, LANES), 0)
    for i, lengths in enumerate((sta, lta)):
        length = jnp.zeros((ROWS, LANES), jnp.int32)
        for c in range(ROWS):
            length = jnp.where(place == c, lengths[me * ROWS + c], length)
        source = iota((ROWS, LANES), 1) - length
        turn[i] = jnp.where(source < 0, source + LANES, source)
        shorter[i] = LANES - length
        scale[i] = 1.0 / length.astype(F32)

    def receive(column, count):
        pltpu.make_async_remote_copy(
            src_ref=ga.at[pl.ds(0, count)], dst_ref=r.at[pl.ds(column * 4, count)], send_sem=send_sem,
            recv_sem=recv_sem.at[column], device_id=(wrap(me + 1, slabs), g), device_id_type=MESH).wait_recv()

    rows = STEP * ROWS

    def compute(i):
        base = i * STEP
        first = (own * 4 + base + 1) % slabs
        place = [wrap(first + n, slabs) for n in range(STEP)]

        def part(o, q):
            return r[pl.ds(base + o, STEP), :, q * LANES : (q + 1) * LANES].reshape(rows, LANES)

        slab = iota((rows, LANES), 0) // ROWS
        follows = jnp.where(slab == wrap(slabs - first, slabs), 0.0, 1.0)
        goes_on = jnp.where(slab == slabs - 1 - first, 0.0, 1.0)
        mine = [part(1, q) for q in range(4)]
        ahead = r[pl.ds(base, 1), :, LANES:].reshape(ROWS, 3 * LANES)
        windows = stack(
            lanes(ahead, mine[0][:ROWS]),
            lanes(part(0, 3) * follows.astype(BF16), *mine[:3]),
            lanes(*mine[1:], part(2, 0) * goes_on.astype(BF16)),
        )
        filtered = dot(windows, toep[...])
        energy = filtered * filtered
        running = dot(lanes(*split(energy, 3)), sums[...])
        high, low = split(filtered[ROWS:], 2)
        spectrum = dot(lanes(high, low, high), table[...])
        power = spectrum[:, :LANES] * spectrum[:, :LANES] + spectrum[:, LANES:] * spectrum[:, LANES:]
        back = running[:ROWS, LANES:]
        left, right = running[ROWS : ROWS + rows], running[ROWS + rows :]
        ups = [left[:, :LANES], left[:, LANES:], right[:, :LANES], right[:, LANES:]]
        before = stack(back, ups[3][: rows - ROWS]) * follows
        downs = [before - before[:, LANES - 1 :], ups[0], ups[1] - ups[1][:, LANES - 1 :], ups[2]]
        lane = iota((rows, LANES), 1)
        means = []
        for i in range(2):
            kept = lane < stack(*[shorter[i]] * STEP)
            inverse = stack(*[scale[i]] * STEP)
            source = stack(*[turn[i]] * STEP)
            means.append([
                (up - jnp.take_along_axis(jnp.where(kept, up, down), source, axis=1)) * inverse
                for up, down in zip(ups, downs)
            ])
        for q in range(4):
            ratio = (means[0][q] / jnp.maximum(means[1][q], 0.5)).astype(BF16)
            for n in range(STEP):
                at = pl.multiple_of(place[n] * 4 * LANES + q * LANES, LANES)
                ratio_out[:, pl.ds(at, LANES)] = ratio[n * ROWS : (n + 1) * ROWS]
        total = dot(lanes(*split(power, 2)), sel[...])
        for n in range(STEP):
            for f in range(2):
                at = pl.multiple_of((place[n] * 2 + f) * ROWS, ROWS)
                begin = f * rows + n * ROWS
                bands[pl.ds(at, ROWS), :] = total[begin : begin + ROWS]

    receive(0, 3)
    r[slabs] = r[0]
    r[slabs + 1] = r[1]

    @pl.loop(0, slabs // STEP)
    def _(i):
        for n in range(STEP // 4):
            column = i * (STEP // 4) + 1 + n

            @pl.when(column < columns)
            def _():
                receive(column, 4)

        compute(i)

    @pl.when(has_hi)
    def _():
        to_hi().wait_send()

    @pl.when(has_lo)
    def _():
        to_lo().wait_send()

    pltpu.make_async_remote_copy(
        src_ref=ga.at[pl.ds(0, slabs - 1)], dst_ref=r.at[pl.ds(0, slabs - 1)], send_sem=send_sem,
        recv_sem=recv_sem.at[0], device_id=(wrap(me + 1, slabs), g), device_id_type=MESH).wait_send()


def body(traces, fir_taps, gauge_half, sta_length, lta_length, band_edges):
    slabs, groups = lax.axis_size("tm"), lax.axis_size("grp")
    chans, local = traces.shape
    taps = fir_taps
    half = gauge_half.reshape(-1, LANES)
    table = jnp.asarray(spectral_table())
    total = slabs * local
    vmem = pl.BlockSpec(memory_space=pltpu.VMEM)
    hbm = pl.BlockSpec(memory_space=pltpu.HBM)
    dma = pltpu.SemaphoreType.DMA
    operands = (traces, taps, half, sta_length, lta_length, band_edges, table)
    operands = [pltpu.with_memory_space_constraint(a, pltpu.HBM) for a in operands]
    ratio, bands, widths = pl.pallas_call(
        functools.partial(kernel, slabs, groups),
        out_shape=(
            jax.ShapeDtypeStruct((ROWS, total), BF16),
            jax.ShapeDtypeStruct((total // FRAME * ROWS, LANES), F32),
            jax.ShapeDtypeStruct((NBANDS, LANES), F32),
        ),
        in_specs=[hbm] * 7,
        out_specs=(vmem, vmem, vmem),
        scratch_shapes=[
            pltpu.VMEM((chans, local), BF16),
            pltpu.VMEM((slabs, ROWS, local), BF16),
            pltpu.VMEM((slabs + 2, ROWS, local), BF16),
            pltpu.VMEM((ROWS, local), BF16),
            pltpu.VMEM((ROWS, local), BF16),
            pltpu.VMEM(taps.shape, taps.dtype),
            pltpu.VMEM(half.shape, half.dtype),
            pltpu.VMEM(table.shape, BF16),
            pltpu.VMEM((2 * FRAME, FRAME), BF16),
            pltpu.VMEM((3 * FRAME, FRAME), BF16),
            pltpu.VMEM((2 * LANES, LANES), BF16),
            pltpu.VMEM((2, ROWS, LANES), jnp.int32),
            pltpu.VMEM((2, ROWS, LANES), jnp.int32),
            pltpu.VMEM((2, ROWS, LANES), F32),
            pltpu.SMEM(sta_length.shape, jnp.int32),
            pltpu.SMEM(lta_length.shape, jnp.int32),
            pltpu.SMEM(band_edges.shape, jnp.int32),
            dma((7,)),
            dma,
            dma((slabs // 4,)),
            dma((2,)),
            dma((2,)),
        ],
        compiler_params=pltpu.CompilerParams(
            collective_id=0, has_side_effects=True, vmem_limit_bytes=40 * 2**20
        ),
        cost_estimate=pl.CostEstimate(flops=4 * 10**9, bytes_accessed=3 * 2**20, transcendentals=0),
    )(*operands)
    frames = total // FRAME
    return pl.pallas_call(
        finish,
        out_shape=(
            jax.ShapeDtypeStruct((1, ROWS, total), BF16),
            jax.ShapeDtypeStruct((1, ROWS, NBANDS, frames), F32),
        ),
        in_specs=[vmem] * 3,
        out_specs=(hbm, hbm),
        scratch_shapes=[pltpu.VMEM((ROWS, NBANDS, frames), F32), dma((2,))],
        compiler_params=pltpu.CompilerParams(vmem_limit_bytes=8 * 2**20),
    )(ratio, bands, widths)


def solution(mesh):
    in_specs = (P("grp", "tm"), P(), P("grp"), P("grp"), P("grp"), P())
    out_specs = (P("grp", "tm", None), P("grp", "tm", None, None))
    return jax.shard_map(body, mesh=mesh, in_specs=in_specs, out_specs=out_specs, check_vma=False)
```

```python
import functools
import math

import jax
import jax.numpy as jnp
import numpy as np
from jax import lax
from jax.experimental import pallas as pl
from jax.experimental.pallas import tpu as pltpu
from jax.sharding import PartitionSpec as P

NTAPS = 129
REACH = 64
LANES = 128
FRAME = 256
NBANDS = 8
ROWS = 16
STEP = 16
MESH = pl.DeviceIdType.MESH
F32 = jnp.float32
BF16 = jnp.bfloat16


def spectral_table():
    n = np.arange(FRAME)
    k = np.arange(FRAME // 2)
    angle = 2.0 * math.pi * ((n[:, None] * k[None, :]) % FRAME) / FRAME
    hann = 0.5 - 0.5 * np.cos(2.0 * math.pi * n / FRAME)
    table = np.concatenate([np.cos(angle), np.sin(angle)], axis=1) * hann[:, None]
    high = table.astype(jnp.bfloat16)
    low = (table - high.astype(np.float64)).astype(jnp.bfloat16)
    return np.concatenate([high, high, low], axis=0)


def iota(shape, dim):
    return lax.broadcasted_iota(jnp.int32, shape, dim)


def split(x, terms):
    parts = []
    for _ in range(terms - 1):
        parts.append(x.astype(BF16))
        x = x - parts[-1].astype(F32)
    return parts + [x.astype(BF16)]


def dot(a, b):
    return jnp.dot(a, b, preferred_element_type=F32)


def lanes(*parts):
    return jnp.concatenate(parts, axis=1)


def stack(*parts):
    return jnp.concatenate(parts, axis=0)


def gauge_matrix(half, width, off):
    n = half.shape[0]
    if width > LANES:
        half = lanes(*[half] * (width // LANES))
    rel = (iota((n, width), 1) - iota((n, width), 0) - off).astype(F32)
    side = jnp.where(jnp.abs(rel) == half, -0.5, 0.0)
    return jnp.where(rel == 0.0, 1.0, side).astype(BF16)


def wrap(i, n):
    return jnp.where(i >= n, i - n, i)


def finish(ratio, bands, widths, ratio_out, sig_out, sig, sems):
    size = ratio.shape[1] // 4
    parts = [
        pltpu.make_async_copy(
            ratio.at[:, pl.ds(i * size, size)], ratio_out.at[0, :, pl.ds(i * size, size)], sems.at[i + 1])
        for i in range(4)
    ]
    for part in parts:
        part.start()
    mean = bands[...].T.reshape(sig.shape) / widths[:, : sig.shape[2]]
    sig[...] = jnp.log1p(mean / FRAME)
    logs = pltpu.make_async_copy(sig, sig_out.at[0], sems.at[0])
    logs.start()
    for part in parts:
        part.wait()
    logs.wait()


def kernel(
    slabs, groups,
    traces, taps_in, half_in, sta_in, lta_in, edges_in, table_in,
    ratio_out, bands, widths,
    x, ga, r, lo_halo, hi_halo, taps, half, table, toep, sums, sel, turn, shorter, scale,
    sta, lta, edges,
    in_sem, send_sem, recv_sem, hsend, hrecv,
):
    me = lax.axis_index("tm")
    g = lax.axis_index("grp")
    chans = x.shape[0]
    block = LANES
    per = block // ROWS
    columns = slabs // 4
    own = me // 4
    has_lo = g > 0
    has_hi = g < groups - 1

    barrier = pltpu.get_barrier_semaphore()

    @pl.loop(1, slabs, unroll=9)
    def _(k):
        pl.semaphore_signal(barrier, inc=1, device_id=(wrap(me + k, slabs), g), device_id_type=MESH)

    @pl.when(has_lo)
    def _():
        pl.semaphore_signal(barrier, inc=1, device_id=(me, g - 1), device_id_type=MESH)

    @pl.when(has_hi)
    def _():
        pl.semaphore_signal(barrier, inc=1, device_id=(me, g + 1), device_id_type=MESH)

    pairs = [(traces, x), (half_in, half), (table_in, table), (taps_in, taps), (sta_in, sta), (lta_in, lta), (edges_in, edges)]
    loads = [pltpu.make_async_copy(a, b, in_sem.at[i]) for i, (a, b) in enumerate(pairs)]
    for load in loads:
        load.start()
    def half_column(i):
        row = jnp.broadcast_to(half[pl.ds(i, 1), :].astype(F32), (LANES, LANES))
        return row.T

    loads[0].wait()
    loads[1].wait()
    width = min(2 * LANES, chans)

    @pl.loop(0, chans // block, unroll=4)
    def _(i):
        start = jnp.clip(i * block - REACH, 0, chans - width)
        rows = x[pl.ds(pl.multiple_of(start, ROWS), width), :]
        m = gauge_matrix(half_column(i), width, i * block - start)
        ga[pl.ds(i * per, per)] = dot(m, rows).astype(BF16).reshape(per, ROWS, x.shape[1])

    neighbours = jnp.where(has_lo, 1, 0) + jnp.where(has_hi, 1, 0)
    pl.semaphore_wait(barrier, slabs - 1 + neighbours)

    def to_hi():
        return pltpu.make_async_remote_copy(
            src_ref=traces.at[pl.ds(chans - ROWS, ROWS)], dst_ref=lo_halo, send_sem=hsend.at[0],
            recv_sem=hrecv.at[0], device_id=(me, g + 1), device_id_type=MESH)

    def to_lo():
        return pltpu.make_async_remote_copy(
            src_ref=traces.at[pl.ds(0, ROWS)], dst_ref=hi_halo, send_sem=hsend.at[1],
            recv_sem=hrecv.at[1], device_id=(me, g - 1), device_id_type=MESH)

    @pl.when(has_hi)
    def _():
        to_hi().start()

    @pl.when(has_lo)
    def _():
        to_lo().start()

    seat = me % 4

    def send(d, back):
        return pltpu.make_async_remote_copy(
            src_ref=ga.at[d], dst_ref=r.at[back * 4 + seat], send_sem=send_sem,
            recv_sem=recv_sem.at[back], device_id=(d, g), device_id_type=MESH)

    across = (own * 2 + 1 - me // 2 % 2) * 2
    beside = (own * 2 + me // 2 % 2) * 2

    def send_column(k, allowed):
        shift = jnp.where(k > own, columns - k, -k) * 4
        for e in range(4):
            d = (across if e < 2 else beside) + shift + e % 2

            @pl.when(allowed(d))
            def _():
                send(d, k).start()

    def on_edge(d):
        return jnp.logical_or(d == 0, d == slabs - 1)

    early = columns // 2

    @pl.loop(0, early)
    def _(k):
        send_column(k, lambda d: jnp.logical_and(d != me, jnp.logical_not(on_edge(d))))

    @pl.when(has_lo)
    def _():
        to_hi().wait_recv()

    @pl.when(jnp.logical_not(has_lo))
    def _():
        lo_halo[...] = jnp.zeros_like(lo_halo)

    @pl.when(has_hi)
    def _():
        to_lo().wait_recv()

    @pl.when(jnp.logical_not(has_hi))
    def _():
        hi_halo[...] = jnp.zeros_like(hi_halo)

    edge = LANES - ROWS
    m = gauge_matrix(half_column(0)[:ROWS], LANES, ROWS)
    ga[0] = dot(m, stack(lo_halo[...], x[0:edge, :])).astype(BF16)
    m = gauge_matrix(half_column(chans // block - 1)[block - ROWS :], LANES, edge - ROWS)
    ga[slabs - 1] = dot(m, stack(x[chans - edge :, :], hi_halo[...])).astype(BF16)

    for d in (0, slabs - 1):
        back = wrap(own + columns - d // 4, columns)

        @pl.when(jnp.logical_and(d != me, back < early))
        def _():
            send(d, back).start()

    @pl.loop(early, columns)
    def _(k):
        send_column(k, lambda d: d != me)

    r[pl.ds(seat, 1)] = ga[pl.ds(me, 1)]
    for load in loads[2:]:
        load.wait()
    tap = taps[...].astype(F32).reshape(1, NTAPS)
    row = jnp.concatenate([tap, jnp.zeros((1, 2 * FRAME - NTAPS), F32)], axis=1)
    row = jnp.broadcast_to(row, (FRAME, 2 * FRAME))
    toep[...] = pltpu.roll(row, REACH, 1, stride=1, stride_axis=0).T.astype(BF16)
    earlier = iota((FRAME, FRAME), 0)
    sample = iota((FRAME, FRAME), 1)
    upto = jnp.where(earlier <= sample, 1.0, 0.0).astype(BF16)
    for i in range(3):
        sums[i * FRAME : (i + 1) * FRAME] = upto
    bins = iota((LANES, LANES), 0)
    band = iota((LANES, LANES), 1)
    select = jnp.zeros((LANES, LANES), F32)
    width_of = jnp.ones((NBANDS, LANES), F32)
    for b in range(NBANDS):
        low, high = edges[b], edges[b + 1]
        inside = jnp.logical_and(band % NBANDS == b, jnp.logical_and(bins >= low, bins < high))
        select = jnp.where(inside, 1.0, select)
        count = jnp.full((NBANDS, LANES), high - low, jnp.int32).astype(F32)
        width_of = jnp.where(iota((NBANDS, LANES), 0) == b, count, width_of)
    for i in range(2):
        sel[i * LANES : (i + 1) * LANES] = select.astype(BF16)
    widths[...] = width_of
    place = iota((ROWS, LANES), 0)
    for i, lengths in enumerate((sta, lta)):
        length = jnp.zeros((ROWS, LANES), jnp.int32)
        for c in range(ROWS):
            length = jnp.where(place == c, lengths[me * ROWS + c], length)
        source = iota((ROWS, LANES), 1) - length
        turn[i] = jnp.where(source < 0, source + LANES, source)
        shorter[i] = LANES - length
        scale[i] = 1.0 / length.astype(F32)

    def receive(column, count):
        pltpu.make_async_remote_copy(
            src_ref=ga.at[pl.ds(0, count)], dst_ref=r.at[pl.ds(column * 4, count)], send_sem=send_sem,
            recv_sem=recv_sem.at[column], device_id=(wrap(me + 1, slabs), g), device_id_type=MESH).wait_recv()

    rows = STEP * ROWS

    def compute(i):
        base = i * STEP
        first = (own * 4 + base + 1) % slabs
        place = [wrap(first + n, slabs) for n in range(STEP)]

        def part(o, q):
            return r[pl.ds(base + o, STEP), :, q * LANES : (q + 1) * LANES].reshape(rows, LANES)

        slab = iota((rows, LANES), 0) // ROWS
        follows = jnp.where(slab == wrap(slabs - first, slabs), 0.0, 1.0)
        goes_on = jnp.where(slab == slabs - 1 - first, 0.0, 1.0)
        mine = [part(1, q) for q in range(4)]
        ahead = r[pl.ds(base, 1), :, LANES:].reshape(ROWS, 3 * LANES)
        windows = stack(
            lanes(ahead, mine[0][:ROWS]),
            lanes(part(0, 3) * follows.astype(BF16), *mine[:3]),
            lanes(*mine[1:], part(2, 0) * goes_on.astype(BF16)),
        )
        filtered = dot(windows, toep[...])
        energy = filtered * filtered
        running = dot(lanes(*split(energy, 3)), sums[...])
        high, low = split(filtered[ROWS:], 2)
        spectrum = dot(lanes(high, low, high), table[...])
        power = spectrum[:, :LANES] * spectrum[:, :LANES] + spectrum[:, LANES:] * spectrum[:, LANES:]
        back = running[:ROWS, LANES:]
        left, right = running[ROWS : ROWS + rows], running[ROWS + rows :]
        ups = [left[:, :LANES], left[:, LANES:], right[:, :LANES], right[:, LANES:]]
        before = stack(back, ups[3][: rows - ROWS]) * follows
        downs = [before - before[:, LANES - 1 :], ups[0], ups[1] - ups[1][:, LANES - 1 :], ups[2]]
        lane = iota((rows, LANES), 1)
        means = []
        for i in range(2):
            kept = lane < stack(*[shorter[i]] * STEP)
            inverse = stack(*[scale[i]] * STEP)
            source = stack(*[turn[i]] * STEP)
            means.append([
                (up - jnp.take_along_axis(jnp.where(kept, up, down), source, axis=1, mode=lax.GatherScatterMode.PROMISE_IN_BOUNDS)) * inverse
                for up, down in zip(ups, downs)
            ])
        for q in range(4):
            ratio = (means[0][q] / jnp.maximum(means[1][q], 0.5)).astype(BF16)
            for n in range(STEP):
                at = pl.multiple_of(place[n] * 4 * LANES + q * LANES, LANES)
                ratio_out[:, pl.ds(at, LANES)] = ratio[n * ROWS : (n + 1) * ROWS]
        total = dot(lanes(*split(power, 2)), sel[...])
        total = jnp.where(iota((2 * rows, LANES), 1) // NBANDS == iota((2 * rows, LANES), 0) % ROWS, total, 0.0)
        total = total.reshape(2 * STEP, ROWS, LANES).sum(axis=1)
        for n in range(STEP):
            for f in range(2):
                bands[pl.ds(place[n] * 2 + f, 1), :] = total[f * STEP + n : f * STEP + n + 1]

    receive(0, 3)
    r[slabs] = r[0]
    r[slabs + 1] = r[1]

    @pl.loop(0, slabs // STEP)
    def _(i):
        for n in range(STEP // 4):
            column = i * (STEP // 4) + 1 + n

            @pl.when(column < columns)
            def _():
                receive(column, 4)

        compute(i)

    @pl.when(has_hi)
    def _():
        to_hi().wait_send()

    @pl.when(has_lo)
    def _():
        to_lo().wait_send()

    pltpu.make_async_remote_copy(
        src_ref=ga.at[pl.ds(0, slabs - 1)], dst_ref=r.at[pl.ds(0, slabs - 1)], send_sem=send_sem,
        recv_sem=recv_sem.at[0], device_id=(wrap(me + 1, slabs), g), device_id_type=MESH).wait_send()


def body(traces, fir_taps, gauge_half, sta_length, lta_length, band_edges):
    slabs, groups = lax.axis_size("tm"), lax.axis_size("grp")
    chans, local = traces.shape
    taps = fir_taps
    half = gauge_half.reshape(-1, LANES)
    table = jnp.asarray(spectral_table())
    total = slabs * local
    vmem = pl.BlockSpec(memory_space=pltpu.VMEM)
    hbm = pl.BlockSpec(memory_space=pltpu.HBM)
    dma = pltpu.SemaphoreType.DMA
    operands = (traces, taps, half, sta_length, lta_length, band_edges, table)
    operands = [pltpu.with_memory_space_constraint(a, pltpu.HBM) for a in operands]
    ratio, bands, widths = pl.pallas_call(
        functools.partial(kernel, slabs, groups),
        out_shape=(
            jax.ShapeDtypeStruct((ROWS, total), BF16),
            jax.ShapeDtypeStruct((total // FRAME, LANES), F32),
            jax.ShapeDtypeStruct((NBANDS, LANES), F32),
        ),
        in_specs=[hbm] * 7,
        out_specs=(vmem, vmem, vmem),
        scratch_shapes=[
            pltpu.VMEM((chans, local), BF16),
            pltpu.VMEM((slabs, ROWS, local), BF16),
            pltpu.VMEM((slabs + 2, ROWS, local), BF16),
            pltpu.VMEM((ROWS, local), BF16),
            pltpu.VMEM((ROWS, local), BF16),
            pltpu.VMEM(taps.shape, taps.dtype),
            pltpu.VMEM(half.shape, half.dtype),
            pltpu.VMEM(table.shape, BF16),
            pltpu.VMEM((2 * FRAME, FRAME), BF16),
            pltpu.VMEM((3 * FRAME, FRAME), BF16),
            pltpu.VMEM((2 * LANES, LANES), BF16),
            pltpu.VMEM((2, ROWS, LANES), jnp.int32),
            pltpu.VMEM((2, ROWS, LANES), jnp.int32),
            pltpu.VMEM((2, ROWS, LANES), F32),
            pltpu.SMEM(sta_length.shape, jnp.int32),
            pltpu.SMEM(lta_length.shape, jnp.int32),
            pltpu.SMEM(band_edges.shape, jnp.int32),
            dma((7,)),
            dma,
            dma((slabs // 4,)),
            dma((2,)),
            dma((2,)),
        ],
        compiler_params=pltpu.CompilerParams(
            collective_id=0, has_side_effects=True, vmem_limit_bytes=40 * 2**20
        ),
        cost_estimate=pl.CostEstimate(flops=4 * 10**9, bytes_accessed=3 * 2**20, transcendentals=0),
    )(*operands)
    frames = total // FRAME
    return pl.pallas_call(
        finish,
        out_shape=(
            jax.ShapeDtypeStruct((1, ROWS, total), BF16),
            jax.ShapeDtypeStruct((1, ROWS, NBANDS, frames), F32),
        ),
        in_specs=[vmem] * 3,
        out_specs=(hbm, hbm),
        scratch_shapes=[pltpu.VMEM((ROWS, NBANDS, frames), F32), dma((5,))],
        compiler_params=pltpu.CompilerParams(vmem_limit_bytes=8 * 2**20),
    )(ratio, bands, widths)


def solution(mesh):
    in_specs = (P("grp", "tm"), P(), P("grp"), P("grp"), P("grp"), P())
    out_specs = (P("grp", "tm", None), P("grp", "tm", None, None))
    return jax.shard_map(body, mesh=mesh, in_specs=in_specs, out_specs=out_specs, check_vma=False)
```

```python
import functools
import math

import jax
import jax.numpy as jnp
import numpy as np
from jax import lax
from jax.experimental import pallas as pl
from jax.experimental.pallas import tpu as pltpu
from jax.sharding import PartitionSpec as P

NTAPS = 129
REACH = 64
LANES = 128
FRAME = 256
NBANDS = 8
ROWS = 16
STEP = 16
MESH = pl.DeviceIdType.MESH
F32 = jnp.float32
BF16 = jnp.bfloat16


def spectral_table():
    n = np.arange(FRAME)
    k = np.arange(FRAME // 2)
    angle = 2.0 * math.pi * ((n[:, None] * k[None, :]) % FRAME) / FRAME
    hann = 0.5 - 0.5 * np.cos(2.0 * math.pi * n / FRAME)
    table = np.concatenate([np.cos(angle), np.sin(angle)], axis=1) * hann[:, None]
    high = table.astype(jnp.bfloat16)
    low = (table - high.astype(np.float64)).astype(jnp.bfloat16)
    return np.concatenate([high, high, low], axis=0)


def iota(shape, dim):
    return lax.broadcasted_iota(jnp.int32, shape, dim)


def split(x, terms):
    parts = []
    for _ in range(terms - 1):
        parts.append(x.astype(BF16))
        x = x - parts[-1].astype(F32)
    return parts + [x.astype(BF16)]


def dot(a, b):
    return jnp.dot(a, b, preferred_element_type=F32)


def lanes(*parts):
    return jnp.concatenate(parts, axis=1)


def stack(*parts):
    return jnp.concatenate(parts, axis=0)


def gauge_matrix(half, width, off):
    n = half.shape[0]
    if width > LANES:
        half = lanes(*[half] * (width // LANES))
    rel = (iota((n, width), 1) - iota((n, width), 0) - off).astype(F32)
    side = jnp.where(jnp.abs(rel) == half, -0.5, 0.0)
    return jnp.where(rel == 0.0, 1.0, side).astype(BF16)


def wrap(i, n):
    return jnp.where(i >= n, i - n, i)


def finish(ratio, bands, widths, ratio_out, sig_out, sig, sems):
    whole = pltpu.make_async_copy(ratio, ratio_out.at[0], sems.at[0])
    whole.start()
    for c in range(ROWS):
        mean = bands[pl.ds(c, sig.shape[2], stride=ROWS), :].T[:NBANDS] / widths[:, : sig.shape[2]]
        sig[c] = jnp.log1p(mean / FRAME)
    logs = pltpu.make_async_copy(sig, sig_out.at[0], sems.at[1])
    logs.start()
    whole.wait()
    logs.wait()


def kernel(
    slabs, groups,
    traces, taps_in, half_in, sta_in, lta_in, edges_in, table_in,
    ratio_out, bands, widths,
    x, ga, r, lo_halo, hi_halo, taps, half, table, toep, sums, sel, turn, shorter, scale,
    sta, lta, edges,
    in_sem, send_sem, recv_sem, hsend, hrecv,
):
    me = lax.axis_index("tm")
    g = lax.axis_index("grp")
    chans = x.shape[0]
    block = LANES
    per = block // ROWS
    columns = slabs // 4
    own = me // 4
    has_lo = g > 0
    has_hi = g < groups - 1

    barrier = pltpu.get_barrier_semaphore()

    @pl.loop(1, slabs, unroll=True)
    def _(k):
        pl.semaphore_signal(barrier, inc=1, device_id=(wrap(me + k, slabs), g), device_id_type=MESH)

    @pl.when(has_lo)
    def _():
        pl.semaphore_signal(barrier, inc=1, device_id=(me, g - 1), device_id_type=MESH)

    @pl.when(has_hi)
    def _():
        pl.semaphore_signal(barrier, inc=1, device_id=(me, g + 1), device_id_type=MESH)

    pairs = [(traces, x), (half_in, half), (table_in, table), (taps_in, taps), (sta_in, sta), (lta_in, lta), (edges_in, edges)]
    loads = [pltpu.make_async_copy(a, b, in_sem.at[i]) for i, (a, b) in enumerate(pairs)]
    for load in loads:
        load.start()
    def half_column(i):
        row = jnp.broadcast_to(half[pl.ds(i, 1), :].astype(F32), (LANES, LANES))
        return row.T

    loads[0].wait()
    loads[1].wait()
    width = min(2 * LANES, chans)

    @pl.loop(0, chans // block, unroll=4)
    def _(i):
        start = jnp.clip(i * block - REACH, 0, chans - width)
        rows = x[pl.ds(pl.multiple_of(start, ROWS), width), :]
        m = gauge_matrix(half_column(i), width, i * block - start)
        ga[pl.ds(i * per, per)] = dot(m, rows).astype(BF16).reshape(per, ROWS, x.shape[1])

    neighbours = jnp.where(has_lo, 1, 0) + jnp.where(has_hi, 1, 0)
    pl.semaphore_wait(barrier, slabs - 1 + neighbours)

    def to_hi():
        return pltpu.make_async_remote_copy(
            src_ref=x.at[pl.ds(chans - ROWS, ROWS)], dst_ref=lo_halo, send_sem=hsend.at[0],
            recv_sem=hrecv.at[0], device_id=(me, g + 1), device_id_type=MESH)

    def to_lo():
        return pltpu.make_async_remote_copy(
            src_ref=x.at[pl.ds(0, ROWS)], dst_ref=hi_halo, send_sem=hsend.at[1],
            recv_sem=hrecv.at[1], device_id=(me, g - 1), device_id_type=MESH)

    @pl.when(has_hi)
    def _():
        to_hi().start()

    @pl.when(has_lo)
    def _():
        to_lo().start()

    seat = me % 4

    def send(d, back):
        return pltpu.make_async_remote_copy(
            src_ref=ga.at[d], dst_ref=r.at[back * 4 + seat], send_sem=send_sem,
            recv_sem=recv_sem.at[back], device_id=(d, g), device_id_type=MESH)

    across = (own * 2 + 1 - me // 2 % 2) * 2
    beside = (own * 2 + me // 2 % 2) * 2

    def send_column(k, allowed):
        shift = jnp.where(k > own, columns - k, -k) * 4
        for e in range(4):
            d = (across if e < 2 else beside) + shift + e % 2

            @pl.when(allowed(d))
            def _():
                send(d, k).start()

    def on_edge(d):
        return jnp.logical_or(d == 0, d == slabs - 1)

    early = columns // 2

    @pl.loop(0, early)
    def _(k):
        send_column(k, lambda d: jnp.logical_and(d != me, jnp.logical_not(on_edge(d))))

    @pl.when(has_lo)
    def _():
        to_hi().wait_recv()

    @pl.when(jnp.logical_not(has_lo))
    def _():
        lo_halo[...] = jnp.zeros_like(lo_halo)

    @pl.when(has_hi)
    def _():
        to_lo().wait_recv()

    @pl.when(jnp.logical_not(has_hi))
    def _():
        hi_halo[...] = jnp.zeros_like(hi_halo)

    edge = LANES - ROWS
    m = gauge_matrix(half_column(0)[:ROWS], LANES, ROWS)
    ga[0] = dot(m, stack(lo_halo[...], x[0:edge, :])).astype(BF16)
    m = gauge_matrix(half_column(chans // block - 1)[block - ROWS :], LANES, edge - ROWS)
    ga[slabs - 1] = dot(m, stack(x[chans - edge :, :], hi_halo[...])).astype(BF16)

    for d in (0, slabs - 1):
        back = wrap(own + columns - d // 4, columns)

        @pl.when(jnp.logical_and(d != me, back < early))
        def _():
            send(d, back).start()

    @pl.loop(early, columns)
    def _(k):
        send_column(k, lambda d: d != me)

    r[pl.ds(seat, 1)] = ga[pl.ds(me, 1)]
    for load in loads[2:]:
        load.wait()
    tap = taps[...].astype(F32).reshape(1, NTAPS)
    row = jnp.concatenate([tap, jnp.zeros((1, 2 * FRAME - NTAPS), F32)], axis=1)
    row = jnp.broadcast_to(row, (FRAME, 2 * FRAME))
    toep[...] = pltpu.roll(row, REACH, 1, stride=1, stride_axis=0).T.astype(BF16)
    earlier = iota((FRAME, FRAME), 0)
    sample = iota((FRAME, FRAME), 1)
    upto = jnp.where(earlier <= sample, 1.0, 0.0).astype(BF16)
    for i in range(3):
        sums[i * FRAME : (i + 1) * FRAME] = upto
    bins = iota((LANES, LANES), 0)
    band = iota((LANES, LANES), 1)
    select = jnp.zeros((LANES, LANES), F32)
    width_of = jnp.ones((NBANDS, LANES), F32)
    for b in range(NBANDS):
        low, high = edges[b], edges[b + 1]
        inside = jnp.logical_and(band == b, jnp.logical_and(bins >= low, bins < high))
        select = jnp.where(inside, 1.0, select)
        count = jnp.full((NBANDS, LANES), high - low, jnp.int32).astype(F32)
        width_of = jnp.where(iota((NBANDS, LANES), 0) == b, count, width_of)
    for i in range(2):
        sel[i * LANES : (i + 1) * LANES] = select.astype(BF16)
    widths[...] = width_of
    place = iota((ROWS, LANES), 0)
    for i, lengths in enumerate((sta, lta)):
        length = jnp.zeros((ROWS, LANES), jnp.int32)
        for c in range(ROWS):
            length = jnp.where(place == c, lengths[me * ROWS + c], length)
        source = iota((ROWS, LANES), 1) - length
        turn[i] = jnp.where(source < 0, source + LANES, source)
        shorter[i] = LANES - length
        scale[i] = 1.0 / length.astype(F32)

    def receive(column, count):
        pltpu.make_async_remote_copy(
            src_ref=ga.at[pl.ds(0, count)], dst_ref=r.at[pl.ds(column * 4, count)], send_sem=send_sem,
            recv_sem=recv_sem.at[column], device_id=(wrap(me + 1, slabs), g), device_id_type=MESH).wait_recv()

    rows = STEP * ROWS

    def compute(i):
        base = i * STEP
        first = (own * 4 + base + 1) % slabs
        place = [wrap(first + n, slabs) for n in range(STEP)]

        def part(o, q):
            return r[pl.ds(base + o, STEP), :, q * LANES : (q + 1) * LANES].reshape(rows, LANES)

        slab = iota((rows, LANES), 0) // ROWS
        follows = jnp.where(slab == wrap(slabs - first, slabs), 0.0, 1.0)
        goes_on = jnp.where(slab == slabs - 1 - first, 0.0, 1.0)
        mine = [part(1, q) for q in range(4)]
        ahead = r[pl.ds(base, 1), :, LANES:].reshape(ROWS, 3 * LANES)
        windows = stack(
            lanes(ahead, mine[0][:ROWS]),
            lanes(part(0, 3) * follows.astype(BF16), *mine[:3]),
            lanes(*mine[1:], part(2, 0) * goes_on.astype(BF16)),
        )
        filtered = dot(windows, toep[...])
        energy = filtered * filtered
        running = dot(lanes(*split(energy, 3)), sums[...])
        high, low = split(filtered[ROWS:], 2)
        spectrum = dot(lanes(high, low, high), table[...])
        power = spectrum[:, :LANES] * spectrum[:, :LANES] + spectrum[:, LANES:] * spectrum[:, LANES:]
        back = running[:ROWS, LANES:]
        left, right = running[ROWS : ROWS + rows], running[ROWS + rows :]
        ups = [left[:, :LANES], left[:, LANES:], right[:, :LANES], right[:, LANES:]]
        before = stack(back, ups[3][: rows - ROWS]) * follows
        downs = [before - before[:, LANES - 1 :], ups[0], ups[1] - ups[1][:, LANES - 1 :], ups[2]]
        lane = iota((rows, LANES), 1)
        means = []
        for i in range(2):
            kept = lane < stack(*[shorter[i]] * STEP)
            inverse = stack(*[scale[i]] * STEP)
            source = stack(*[turn[i]] * STEP)
            means.append([
                (up - jnp.take_along_axis(jnp.where(kept, up, down), source, axis=1)) * inverse
                for up, down in zip(ups, downs)
            ])
        for q in range(4):
            ratio = (means[0][q] / jnp.maximum(means[1][q], 0.5)).astype(BF16)
            for n in range(STEP):
                at = pl.multiple_of(place[n] * 4 * LANES + q * LANES, LANES)
                ratio_out[:, pl.ds(at, LANES)] = ratio[n * ROWS : (n + 1) * ROWS]
        total = dot(lanes(*split(power, 2)), sel[...])
        for n in range(STEP):
            for f in range(2):
                at = pl.multiple_of((place[n] * 2 + f) * ROWS, ROWS)
                begin = f * rows + n * ROWS
                bands[pl.ds(at, ROWS), :] = total[begin : begin + ROWS]

    receive(0, 3)
    r[slabs] = r[0]
    r[slabs + 1] = r[1]

    @pl.loop(0, slabs // STEP)
    def _(i):
        for n in range(STEP // 4):
            column = i * (STEP // 4) + 1 + n

            @pl.when(column < columns)
            def _():
                receive(column, 4)

        compute(i)

    @pl.when(has_hi)
    def _():
        to_hi().wait_send()

    @pl.when(has_lo)
    def _():
        to_lo().wait_send()

    pltpu.make_async_remote_copy(
        src_ref=ga.at[pl.ds(0, slabs - 1)], dst_ref=r.at[pl.ds(0, slabs - 1)], send_sem=send_sem,
        recv_sem=recv_sem.at[0], device_id=(wrap(me + 1, slabs), g), device_id_type=MESH).wait_send()


def body(traces, fir_taps, gauge_half, sta_length, lta_length, band_edges):
    slabs, groups = lax.axis_size("tm"), lax.axis_size("grp")
    chans, local = traces.shape
    taps = fir_taps
    half = gauge_half.reshape(-1, LANES)
    table = jnp.asarray(spectral_table())
    total = slabs * local
    vmem = pl.BlockSpec(memory_space=pltpu.VMEM)
    hbm = pl.BlockSpec(memory_space=pltpu.HBM)
    dma = pltpu.SemaphoreType.DMA
    operands = (traces, taps, half, sta_length, lta_length, band_edges, table)
    operands = [pltpu.with_memory_space_constraint(a, pltpu.HBM) for a in operands]
    ratio, bands, widths = pl.pallas_call(
        functools.partial(kernel, slabs, groups),
        out_shape=(
            jax.ShapeDtypeStruct((ROWS, total), BF16),
            jax.ShapeDtypeStruct((total // FRAME * ROWS, LANES), F32),
            jax.ShapeDtypeStruct((NBANDS, LANES), F32),
        ),
        in_specs=[hbm] * 7,
        out_specs=(vmem, vmem, vmem),
        scratch_shapes=[
            pltpu.VMEM((chans, local), BF16),
            pltpu.VMEM((slabs, ROWS, local), BF16),
            pltpu.VMEM((slabs + 2, ROWS, local), BF16),
            pltpu.VMEM((ROWS, local), BF16),
            pltpu.VMEM((ROWS, local), BF16),
            pltpu.VMEM(taps.shape, taps.dtype),
            pltpu.VMEM(half.shape, half.dtype),
            pltpu.VMEM(table.shape, BF16),
            pltpu.VMEM((2 * FRAME, FRAME), BF16),
            pltpu.VMEM((3 * FRAME, FRAME), BF16),
            pltpu.VMEM((2 * LANES, LANES), BF16),
            pltpu.VMEM((2, ROWS, LANES), jnp.int32),
            pltpu.VMEM((2, ROWS, LANES), jnp.int32),
            pltpu.VMEM((2, ROWS, LANES), F32),
            pltpu.SMEM(sta_length.shape, jnp.int32),
            pltpu.SMEM(lta_length.shape, jnp.int32),
            pltpu.SMEM(band_edges.shape, jnp.int32),
            dma((7,)),
            dma,
            dma((slabs // 4,)),
            dma((2,)),
            dma((2,)),
        ],
        compiler_params=pltpu.CompilerParams(
            collective_id=0, has_side_effects=True, vmem_limit_bytes=40 * 2**20
        ),
        cost_estimate=pl.CostEstimate(flops=4 * 10**9, bytes_accessed=3 * 2**20, transcendentals=0),
    )(*operands)
    frames = total // FRAME
    return pl.pallas_call(
        finish,
        out_shape=(
            jax.ShapeDtypeStruct((1, ROWS, total), BF16),
            jax.ShapeDtypeStruct((1, ROWS, NBANDS, frames), F32),
        ),
        in_specs=[vmem] * 3,
        out_specs=(hbm, hbm),
        scratch_shapes=[pltpu.VMEM((ROWS, NBANDS, frames), F32), dma((2,))],
        compiler_params=pltpu.CompilerParams(vmem_limit_bytes=8 * 2**20),
    )(ratio, bands, widths)


def solution(mesh):
    in_specs = (P("grp", "tm"), P(), P("grp"), P("grp"), P("grp"), P())
    out_specs = (P("grp", "tm", None), P("grp", "tm", None, None))
    return jax.shard_map(body, mesh=mesh, in_specs=in_specs, out_specs=out_specs, check_vma=False)
```
